32 devices in a mesh: space: 4 (over z), scene: 8 (over y, x, core).
Axes of the slice: x: 2, y: 2, z: 4, core: 2. Of those that a mesh axis runs over, the one named last changes fastest.
Arguments:
- pixels: bfloat16 [16, 64, 64, 384], P('scene', 'space'), may hold values from -6 to 6
- dw_kernel: bfloat16 [7, 7, 384], replicated, may hold values from -0.875 to 0.875
- dw_bias: float32 [384], replicated, may hold values from -3 to 3
- norm_gain: float32 [384], replicated, may hold values from 0.25 to 1.75
- w_expand: bfloat16 [384, 1536], replicated, may hold values from -0.3125 to 0.3125
- w_reduce: bfloat16 [1536, 384], replicated, may hold values from -0.15625 to 0.15625
- layer_scale: float32 [384], replicated, may hold values from 0.3 to 1
- pixel_slot: int32 [16, 64, 64], P('scene', 'space'), may hold values from 0 to 63
- intersection: int32 [32, 64], P(('space', 'scene')), may hold values from 0 to 2047, as said below
- parcel_pos: int32 [2048], replicated, may hold values from 0 to 2047, as said below
- parcel_embed: bfloat16 [2048, 384], P(('space', 'scene')), may hold values from -6 to 6
- attn_gain: float32 [384], replicated, may hold values from 0.25 to 1.75
- w_qkv: bfloat16 [384, 1152], replicated, may hold values from -0.91855865 to 0.91855865
- w_out: bfloat16 [384, 384], replicated, may hold values from -0.3125 to 0.3125
- w_class: bfloat16 [384, 20], replicated, may hold values from -10.7165176 to 10.7165176
- labels: int32 [2048], P(('space', 'scene')), may hold values from 0 to 19
Outputs:
- features: bfloat16 [16, 64, 64, 384], P('scene', 'space')
- parcel_state: bfloat16 [2048, 384], P(('space', 'scene'))
- loss: float32 [2048], P(('space', 'scene'))
The draws below stay inside these ranges and needn't reach their ends.
Inputs may be any that keep to these rules, and one draw needn't show every extreme that they name: `intersection`: row t lists 64 distinct parcels; each owner (positions o * 64 to o * 64 + 63) holds 1 to 3 of them, and in every tile some owner holds exactly 3. `parcel_pos`: each position occurs once.
All inputs are finite; a program needn't handle non-finite values.
Results may differ from the reference program's by a relative error of at most 0.035.
The reference program's roundings to bfloat16 on the way (of `normed`, `hidden`, `attn_in`, `queries`, `keys`, `values`, `attended` and `class_in`) count: a program that leaves them out, or rounds other values in their place, can miss the bound.
Values may be sent and summed in bfloat16 or wider, within the bound.
No kernel may reach another device: no remote copies, remote signals or barrier semaphores. Data moves between devices by JAX's collectives and lax.ppermute only.
A program may use at most 128 MiB of HBM per device.

```python
import math
import jax
import jax.numpy as jnp
from jax import lax

C = 384
HID = 1536
KSZ = 7
SCN_DEV = 2
ROWS_DEV = 16
WIDTH_PX = 64
PAR_DEV = 64
HEADS = 6
HEAD_DIM = 64
CLASSES = 20
TILES = 32
K_TILE = 64
PARCELS = 2048
SCENES = 16
ROWS = 64
N_SCENE = 8


def ownership(key):
    base_key = jax.random.fold_in(key, 7)
    pos_perm = jax.random.permutation(jax.random.fold_in(base_key, 1), PARCELS).astype(jnp.int32)
    inverse = jnp.zeros((PARCELS,), jnp.int32).at[pos_perm].set(jnp.arange(PARCELS, dtype=jnp.int32))

    def one_tile(tile_index):
        tile_key = jax.random.fold_in(base_key, tile_index + 2)
        subkeys = jax.random.split(tile_key, 4)
        owner_order = jax.random.permutation(subkeys[0], TILES).astype(jnp.int32)
        first_load = jax.random.randint(subkeys[1], (TILES // 2,), 1, 4).astype(jnp.int32)
        first_load = first_load.at[0].set(3)
        paired = jnp.stack([first_load, 4 - first_load], axis=1).reshape(-1)
        load_count = jnp.zeros((TILES,), jnp.int32).at[owner_order].set(paired)
        owner_dev = jnp.repeat(jnp.arange(TILES, dtype=jnp.int32), load_count, total_repeat_length=K_TILE)
        starts = jnp.cumsum(load_count) - load_count
        slot_rank = jnp.arange(K_TILE, dtype=jnp.int32) - starts[owner_dev]
        offset = jax.random.randint(subkeys[2], (TILES,), 0, PAR_DEV).astype(jnp.int32)
        local_row = (offset[owner_dev] + slot_rank * (PAR_DEV // 3)) % PAR_DEV
        position = owner_dev * PAR_DEV + local_row
        shuffle = jax.random.permutation(subkeys[3], K_TILE)
        return inverse[position[shuffle]]
    intersection = jax.vmap(one_tile)(jnp.arange(TILES, dtype=jnp.int32))
    return (pos_perm, intersection.astype(jnp.int32))


def draw_intersection(key, part):
    return ownership(key)[1]


def draw_parcel_pos(key, part):
    return ownership(key)[0]


def draw_w_qkv(key, part):
    spread = jax.random.uniform(jax.random.fold_in(key, 11), (C, 3 * C), jnp.float32, -1.7, 1.7) * C ** (-0.5)
    return spread.astype(jnp.bfloat16)


def draw_w_class(key, part):
    spread = jax.random.uniform(jax.random.fold_in(key, 13), (C, CLASSES), jnp.float32, -1.7, 1.7) * (4.0 * C ** (-0.5))
    return spread.astype(jnp.bfloat16)


def place_ends(array, key, least, top_value):
    place = [jax.random.randint(jax.random.fold_in(key, axis), (), 0, length) for axis, length in enumerate(array.shape)]
    longest = array.shape.index(max(array.shape))
    neighbour = place[:longest] + [(place[longest] + 1) % array.shape[longest]] + place[longest + 1:]
    return array.at[tuple(place)].set(least).at[tuple(neighbour)].set(top_value)


def levels(stream_key, extent, cuts, least, high):
    factor_of = 1.0
    for dim, parts in cuts:
        draws = jax.random.uniform(jax.random.fold_in(jax.random.fold_in(stream_key, 6), dim), (parts,), jnp.float32, least / len(cuts), high / len(cuts))
        factor_of = factor_of * jnp.repeat(jnp.exp(draws), extent[dim] // parts).reshape((-1,) + (1,) * (len(extent) - 1 - dim))
    return factor_of


def centred(own_key, dims, width, bound, shards=(), kind=jnp.bfloat16):
    drawn = jax.random.normal(own_key, dims, jnp.float32) * width
    if len(shards) > 0:
        drawn = levels(own_key, dims, shards, -0.22, 0.18) * drawn
    return jnp.clip(drawn, min=-bound, max=bound).astype(kind)


def setup_inputs(seed: int = 0) -> dict:
    seeds = jax.random.split(jax.random.key(seed), 17)
    return {
        "pixels": centred(seeds[0], (SCENES, ROWS, WIDTH_PX, C), 1.0, 6.0, ((0, 8), (1, 4))),
        "dw_kernel": centred(seeds[1], (KSZ, KSZ, C), (KSZ * KSZ) ** -0.5, 0.875),
        "dw_bias": centred(seeds[2], (C,), 0.5, 3.0, (), jnp.float32),
        "norm_gain": jnp.clip(1.0 + 0.15 * jax.random.normal(seeds[3], (C,), jnp.float32), 0.25, 1.75),
        "w_expand": centred(seeds[4], (C, HID), C ** -0.5, 0.3125),
        "w_reduce": centred(seeds[5], (HID, C), HID ** -0.5, 0.15625),
        "layer_scale": jnp.clip(jnp.exp(jax.random.uniform(seeds[6], (C,), jnp.float32, math.log(0.3), math.log(1.0))), 0.3, 1.0),
        "pixel_slot": place_ends(jax.random.randint(seeds[7], (SCENES, ROWS, WIDTH_PX), 0, K_TILE), jax.random.fold_in(seeds[7], 1), 0, K_TILE - 1).astype(jnp.int32),
        "intersection": draw_intersection(jax.random.fold_in(seeds[16], 71), 0),
        "parcel_pos": draw_parcel_pos(jax.random.fold_in(seeds[16], 71), 0),
        "parcel_embed": centred(seeds[10], (PARCELS, C), 1.0, 6.0, ((0, 32),)),
        "attn_gain": jnp.clip(1.0 + 0.15 * jax.random.normal(seeds[11], (C,), jnp.float32), 0.25, 1.75),
        "w_qkv": draw_w_qkv(jax.random.fold_in(seeds[16], 71), 0),
        "w_out": centred(seeds[13], (C, C), C ** -0.5, 0.3125),
        "w_class": draw_w_class(jax.random.fold_in(seeds[16], 71), 0),
        "labels": place_ends(jax.random.randint(seeds[15], (PARCELS,), 0, CLASSES), jax.random.fold_in(seeds[15], 1), 0, CLASSES - 1).astype(jnp.int32),
    }


epsilon = 1e-06

def layer_norm(values):
    average = lax.optimization_barrier(jnp.mean(values, axis=-1, keepdims=True))
    centered = values - average
    return centered * lax.rsqrt(lax.optimization_barrier(jnp.mean(centered * centered, axis=-1, keepdims=True)) + epsilon)

def convnext_block(padded, center, dw_kernel, dw_bias, norm_gain, w_expand, w_reduce, layer_scale):
    height = center.shape[1]
    breadth = center.shape[2]
    kernel_f32 = dw_kernel.astype(jnp.float32)
    spatial = jnp.zeros(center.shape, jnp.float32)
    for row_off in range(dw_kernel.shape[0]):
        for col_off in range(dw_kernel.shape[1]):
            window = padded[:, row_off:row_off + height, col_off:col_off + breadth, :]
            spatial = spatial + window.astype(jnp.float32) * kernel_f32[row_off, col_off]
    spatial = spatial + dw_bias
    normed = (layer_norm(spatial) * norm_gain).astype(jnp.bfloat16)
    channels = center.shape[-1]
    flattened = normed.reshape(-1, channels)
    hidden = jax.nn.gelu(jnp.dot(flattened, w_expand, preferred_element_type=jnp.float32), approximate=False).astype(jnp.bfloat16)
    branch = jnp.dot(hidden, w_reduce, preferred_element_type=jnp.float32).reshape(center.shape)
    return (center.astype(jnp.float32) + layer_scale * branch).astype(jnp.bfloat16)

def reference(pixels, dw_kernel, dw_bias, norm_gain, w_expand, w_reduce, layer_scale, pixel_slot, intersection, parcel_pos, parcel_embed, attn_gain, w_qkv, w_out, w_class, labels):

    def one_scene(scene_map):
        padded = jnp.pad(scene_map, ((3, 3), (3, 3), (0, 0)))[None]
        return convnext_block(padded, scene_map[None], dw_kernel, dw_bias, norm_gain, w_expand, w_reduce, layer_scale)[0]
    features = lax.map(one_scene, pixels)
    anchor = jnp.zeros((), jnp.int32)

    def pool_tile(tile_index, running):
        parcel_table, totals = running
        tile_index = jnp.asarray(tile_index).astype(jnp.int32)
        space_index = tile_index // N_SCENE
        scene_index = tile_index % N_SCENE
        first_scene = (scene_index * SCN_DEV).astype(jnp.int32)
        first_row = (space_index * ROWS_DEV).astype(jnp.int32)
        tile_block = lax.dynamic_slice(features, (first_scene, first_row, anchor, anchor), (SCN_DEV, ROWS_DEV, WIDTH_PX, C))
        slot_block = lax.dynamic_slice(pixel_slot, (first_scene, first_row, anchor), (SCN_DEV, ROWS_DEV, WIDTH_PX)).reshape(-1)
        membership = (jnp.arange(K_TILE, dtype=jnp.int32)[:, None] == slot_block[None, :]).astype(jnp.bfloat16)
        slot_sums = jnp.dot(membership, tile_block.reshape(-1, C), preferred_element_type=jnp.float32)
        slot_counts = lax.optimization_barrier(jnp.sum(membership.astype(jnp.float32), axis=1))
        parcels_here = lax.dynamic_index_in_dim(intersection, tile_index, 0, keepdims=False)
        positions = jnp.take(parcel_pos, parcels_here)
        return (parcel_table.at[positions].add(slot_sums), totals.at[positions].add(slot_counts))
    parcel_table, totals = lax.fori_loop(0, TILES, pool_tile, (jnp.zeros((PARCELS, C), jnp.float32), jnp.zeros((PARCELS,), jnp.float32)))
    tokens = parcel_table / jnp.maximum(totals, 1.0)[:, None] + parcel_embed.astype(jnp.float32)
    attn_in = (layer_norm(tokens) * attn_gain).astype(jnp.bfloat16)
    projected = jnp.dot(attn_in, w_qkv, preferred_element_type=jnp.float32)
    queries = lax.optimization_barrier((projected[:, :C] * HEAD_DIM ** (-0.5)).astype(jnp.bfloat16))
    key_value = lax.optimization_barrier(projected[:, C:].astype(jnp.bfloat16))
    keys = key_value[:, :C].astype(jnp.float32).reshape(PARCELS, HEADS, HEAD_DIM)
    values = key_value[:, C:].astype(jnp.float32).reshape(PARCELS, HEADS, HEAD_DIM)

    def attend(query_block):
        query_f32 = query_block.astype(jnp.float32)
        scores = jnp.einsum('qhd,khd->hqk', query_f32, keys)
        top_score = lax.optimization_barrier(jnp.max(scores, axis=-1, keepdims=True))
        weights = jnp.exp(scores - top_score)
        row_total = lax.optimization_barrier(jnp.sum(weights, axis=-1))
        rounded = lax.optimization_barrier(weights.astype(jnp.bfloat16)).astype(jnp.float32)
        mixed_heads = jnp.einsum('hqk,khd->qhd', rounded, values)
        return mixed_heads / jnp.transpose(row_total)[:, :, None]
    attended = lax.map(attend, queries.reshape(TILES, PAR_DEV, HEADS, HEAD_DIM))
    attended = attended.reshape(PARCELS, C).astype(jnp.bfloat16)
    parcel_out = tokens + jnp.dot(attended, w_out, preferred_element_type=jnp.float32)
    class_in = layer_norm(parcel_out).astype(jnp.bfloat16)
    logits = jnp.dot(class_in, w_class, preferred_element_type=jnp.float32)
    top_logit = lax.optimization_barrier(jnp.max(logits, axis=-1, keepdims=True))
    log_total = top_logit[:, 0] + jnp.log(lax.optimization_barrier(jnp.sum(jnp.exp(logits - top_logit), axis=-1)))
    picked = lax.optimization_barrier(jnp.sum(jnp.where(jnp.arange(CLASSES, dtype=jnp.int32)[None, :] == labels[:, None], logits, 0.0), axis=-1))
    return (features, parcel_out.astype(jnp.bfloat16), log_total - picked)
```

```python
import functools

import jax
import jax.numpy as jnp
from jax import lax
from jax.experimental import pallas as pl
from jax.experimental.pallas import tpu as pltpu
from jax.sharding import PartitionSpec as P

CAP = 3
PAR_DEV = 64
HEADS = 6
HEAD_DIM = 64
BLOCK_ROWS = 4
MARGIN = 8
LANES = 128
EPS = 1e-06
VMEM_LIMIT = 56 * 1024 * 1024
AXES = ("space", "scene")
HIGHEST = lax.Precision.HIGHEST

ERF_Q = (
    0.7978842161181501,
    0.03633428350265726,
    -3.312998427216715e-05,
    -5.524016139049459e-05,
    3.969109860672752e-06,
    -1.334464341485976e-07,
    1.8056169652228524e-09,
)
ERF_U = 30.25


def gelu(x):
    u = jnp.minimum(x * x, ERF_U)
    q = jnp.full_like(u, ERF_Q[-1])
    for coef in ERF_Q[-2::-1]:
        q = q * u + coef
    half = 0.5 * x
    return half + half * jnp.tanh(x * q)


def layer_norm(values):
    average = jnp.mean(values, axis=-1, keepdims=True)
    centered = values - average
    return centered * lax.rsqrt(jnp.mean(centered * centered, axis=-1, keepdims=True) + EPS)


def to_column(row, rows):
    n = row.shape[1]
    same = lax.broadcasted_iota(jnp.int32, (n, n), 0) == lax.broadcasted_iota(jnp.int32, (n, n), 1)
    return jnp.sum(jnp.where(same, jnp.broadcast_to(row, (n, n)), 0), axis=1, keepdims=True)


def to_row(column):
    n = column.shape[0]
    same = lax.broadcasted_iota(jnp.int32, (n, n), 0) == lax.broadcasted_iota(jnp.int32, (n, n), 1)
    return jnp.sum(jnp.where(same, jnp.broadcast_to(column, (n, n)), 0), axis=0, keepdims=True)


def conv_block(source, slab, spat, wb, bias_ref, width):
    chans = spat.shape[1]
    blocks = chans // LANES
    ksz = len(source) - BLOCK_ROWS + 1
    reach = ksz // 2
    for i, row in enumerate(source):
        value = row().astype(jnp.float32)
        for cb in range(blocks):
            slab[cb, i, MARGIN : MARGIN + width, :] = value[:, cb * LANES : (cb + 1) * LANES]
    step = 16
    for cb in range(blocks):
        lane = slice(cb * LANES, (cb + 1) * LANES)
        bias = bias_ref[0:1, lane]
        for col in range(0, width, step):
            total = jnp.zeros((BLOCK_ROWS, step, LANES), jnp.float32)
            for b in range(ksz):
                start = MARGIN - reach + b + col
                for a in range(ksz):
                    tap = wb[cb, a * ksz + b]
                    window = slab[cb, a : a + BLOCK_ROWS, start : start + step, :]
                    total = total + window * jnp.concatenate([tap] * (step // 8), axis=0)[None]
            for r in range(BLOCK_ROWS):
                spat[r * width + col : r * width + col + step, lane] = total[r] + bias


def mlp_block(spat, gain_ref, we_ref, wr_ref, scale_ref, center):
    normed = (layer_norm(spat[...]) * gain_ref[...]).astype(jnp.bfloat16)
    hid = we_ref.shape[1]
    chunk = min(512, hid)
    branch = None
    for start in range(0, hid, chunk):
        pre = jnp.dot(normed, we_ref[:, start : start + chunk], preferred_element_type=jnp.float32)
        part = jnp.dot(
            gelu(pre).astype(jnp.bfloat16),
            wr_ref[start : start + chunk, :],
            preferred_element_type=jnp.float32,
        )
        branch = part if branch is None else branch + part
    return (center.astype(jnp.float32) + scale_ref[...] * branch).astype(jnp.bfloat16)


def prepare(slab, wb, dwk_ref, width):
    slab[:, :, 0:MARGIN, :] = jnp.zeros(slab.shape[:2] + (MARGIN, LANES), jnp.float32)
    slab[:, :, MARGIN + width :, :] = jnp.zeros(slab.shape[:2] + (MARGIN, LANES), jnp.float32)
    taps = dwk_ref.shape[0]
    kernel = dwk_ref[...].astype(jnp.float32)
    for cb in range(wb.shape[0]):
        for t in range(taps):
            wb[cb, t] = jnp.broadcast_to(
                kernel[t : t + 1, cb * LANES : (cb + 1) * LANES], (8, LANES)
            )


def pool(member, feats, sums_ref, counts_ref):
    sums_ref[...] += jnp.dot(member, feats, preferred_element_type=jnp.float32)
    ones = jnp.ones((member.shape[1], LANES), jnp.bfloat16)
    counts_ref[...] += jnp.dot(member, ones, preferred_element_type=jnp.float32)


def membership(slot_ref, scene, row0, width, slots):
    pieces = []
    for r in range(BLOCK_ROWS):
        one = slot_ref[scene, pl.ds(row0 + r, 1), :]
        index = lax.broadcasted_iota(jnp.int32, (slots, width), 0)
        pieces.append((index == one).astype(jnp.float32).astype(jnp.bfloat16))
    return jnp.concatenate(pieces, axis=1)


def inner_kernel(
    rows, slots, x_ref, slot_ref, dwk_ref, bias_ref, gain_ref, we_ref, wr_ref, scale_ref,
    feat_ref, sums_ref, counts_ref, slab, spat, wb,
):
    width = x_ref.shape[2]
    scene = pl.program_id(0)
    ksz = slab.shape[1] - BLOCK_ROWS + 1
    reach = ksz // 2

    @pl.when(scene == 0)
    def _():
        prepare(slab, wb, dwk_ref, width)
        sums_ref[...] = jnp.zeros_like(sums_ref)
        counts_ref[...] = jnp.zeros_like(counts_ref)

    for n, row0 in enumerate(range(BLOCK_ROWS, rows - BLOCK_ROWS, BLOCK_ROWS)):
        source = [
            functools.partial(lambda r: x_ref[scene, r], row0 - reach + i)
            for i in range(BLOCK_ROWS + ksz - 1)
        ]
        conv_block(source, slab, spat, wb, bias_ref, width)
        center = x_ref[scene, row0 : row0 + BLOCK_ROWS].reshape(BLOCK_ROWS * width, -1)
        feats = mlp_block(spat, gain_ref, we_ref, wr_ref, scale_ref, center)
        feat_ref[scene, row0 : row0 + BLOCK_ROWS] = feats.reshape(BLOCK_ROWS, width, -1)
        pool(membership(slot_ref, scene, row0, width, slots), feats, sums_ref, counts_ref)


def edge_kernel(
    rows, slots, owners, x_ref, top_ref, bot_ref, slot_ref, dwk_ref, bias_ref, gain_ref, we_ref,
    wr_ref, scale_ref, feat_in, sums_in, counts_in, inter_ref, pos_ref,
    feat_ref, sent_ref, slab, spat, wb, sums_ref, counts_ref,
):
    width = x_ref.shape[2]
    scene = pl.program_id(0)
    ksz = slab.shape[1] - BLOCK_ROWS + 1
    reach = ksz // 2

    @pl.when(scene == 0)
    def _():
        prepare(slab, wb, dwk_ref, width)
        sums_ref[...] = sums_in[...]
        counts_ref[...] = counts_in[...]
        feat_ref[:, BLOCK_ROWS : rows - BLOCK_ROWS] = feat_in[:, BLOCK_ROWS : rows - BLOCK_ROWS]

    for row0 in (0, rows - BLOCK_ROWS):
        source = []
        for i in range(BLOCK_ROWS + ksz - 1):
            r = row0 - reach + i
            if r < 0:
                source.append(functools.partial(lambda r: top_ref[scene, r], r + reach))
            elif r >= rows:
                source.append(functools.partial(lambda r: bot_ref[scene, r], r - rows))
            else:
                source.append(functools.partial(lambda r: x_ref[scene, r], r))
        conv_block(source, slab, spat, wb, bias_ref, width)
        center = x_ref[scene, row0 : row0 + BLOCK_ROWS].reshape(BLOCK_ROWS * width, -1)
        feats = mlp_block(spat, gain_ref, we_ref, wr_ref, scale_ref, center)
        feat_ref[scene, row0 : row0 + BLOCK_ROWS] = feats.reshape(BLOCK_ROWS, width, -1)
        pool(membership(slot_ref, scene, row0, width, slots), feats, sums_ref, counts_ref)

    @pl.when(scene == pl.num_programs(0) - 1)
    def _():
        parcels = pos_ref.shape[1]
        listed = to_column(inter_ref[...], slots)
        number = lax.broadcasted_iota(jnp.int32, (slots, parcels), 1)
        position = jnp.sum(
            jnp.where(number == listed, jnp.broadcast_to(pos_ref[...], (slots, parcels)), 0),
            axis=1, keepdims=True,
        )
        owner = position // PAR_DEV
        owner_row = to_row(owner)
        this = lax.broadcasted_iota(jnp.int32, (slots, slots), 0)
        other = lax.broadcasted_iota(jnp.int32, (slots, slots), 1)
        rank = jnp.sum(
            jnp.where((owner == owner_row) & (other < this), 1, 0), axis=1, keepdims=True
        )
        place = to_row(rank * owners + owner)
        place_index = lax.broadcasted_iota(jnp.int32, (CAP * owners, slots), 0)
        placer = (place_index == place).astype(jnp.float32)
        sent = jnp.dot(placer, sums_ref[...], precision=HIGHEST, preferred_element_type=jnp.float32)
        local_row = (position - owner * PAR_DEV).astype(jnp.float32)
        lane = lax.broadcasted_iota(jnp.int32, (slots, LANES), 1)
        counts_rows = jnp.where(lane < CAP, counts_ref[...], jnp.broadcast_to(local_row, (slots, LANES)))
        meta = jnp.dot(placer, counts_rows, precision=HIGHEST, preferred_element_type=jnp.float32)
        chans = sent.shape[1]
        lane = lax.broadcasted_iota(jnp.int32, (owners, LANES), 1)
        packed = jnp.zeros((owners, LANES), jnp.float32)
        for k in range(CAP):
            sent_ref[:, k * chans : (k + 1) * chans] = sent[k * owners : (k + 1) * owners]
            packed = jnp.where(
                (lane == k) | (lane == CAP + k), meta[k * owners : (k + 1) * owners], packed
            )
        sent_ref[:, CAP * chans :] = packed


def owner_kernel(recv_ref, embed_ref, gain_ref, tokens_ref, attn_ref):
    chans = embed_ref.shape[1]
    meta = recv_ref[:, CAP * chans :]
    tiles = recv_ref.shape[0]
    sums = jnp.zeros(tokens_ref.shape, jnp.float32)
    counts = jnp.zeros((PAR_DEV, LANES), jnp.float32)
    index = lax.broadcasted_iota(jnp.int32, (PAR_DEV, tiles), 0).astype(jnp.float32)
    for k in range(CAP):
        rows = jnp.broadcast_to(meta[:, CAP + k : CAP + k + 1], (tiles, LANES)).T[0:1, :]
        table = (index == rows).astype(jnp.float32)
        sums += jnp.dot(
            table, recv_ref[:, k * chans : (k + 1) * chans],
            precision=HIGHEST, preferred_element_type=jnp.float32,
        )
        many = jnp.broadcast_to(meta[:, k : k + 1], (tiles, LANES))
        counts += jnp.dot(table, many, precision=HIGHEST, preferred_element_type=jnp.float32)
    tokens = sums / jnp.maximum(counts[:, :1], 1.0) + embed_ref[...].astype(jnp.float32)
    tokens_ref[...] = tokens
    attn_ref[...] = (layer_norm(tokens) * gain_ref[...]).astype(jnp.bfloat16)


def attend_kernel(
    tokens_ref, own_ref, all_ref, wqkv_ref, wout_ref, wclass_ref, labels_ref,
    state_ref, loss_ref, keys, values,
):
    chans = own_ref.shape[1]
    parcels = all_ref.shape[0]
    chunk = min(512, parcels)
    for start in range(0, parcels, chunk):
        part = all_ref[start : start + chunk]
        keys[start : start + chunk] = jnp.dot(
            part, wqkv_ref[:, chans : 2 * chans], preferred_element_type=jnp.float32
        ).astype(jnp.bfloat16)
        values[start : start + chunk] = jnp.dot(
            part, wqkv_ref[:, 2 * chans :], preferred_element_type=jnp.float32
        ).astype(jnp.bfloat16)
    queries = (
        jnp.dot(own_ref[...], wqkv_ref[:, :chans], preferred_element_type=jnp.float32)
        * HEAD_DIM ** (-0.5)
    )
    here = queries.shape[0]
    outs = []
    lane = lax.broadcasted_iota(jnp.int32, (here, chans), 1)
    for h in range(HEADS):
        mask = (lane >= h * HEAD_DIM) & (lane < (h + 1) * HEAD_DIM)
        q = jnp.where(mask, queries, 0.0).astype(jnp.bfloat16)
        scores = lax.dot_general(
            q, keys[...], (((1,), (1,)), ((), ())), preferred_element_type=jnp.float32
        )
        top = jnp.max(scores, axis=1, keepdims=True)
        weights = jnp.exp(scores - top)
        total = jnp.sum(weights, axis=1, keepdims=True)
        mixed = jnp.dot(
            weights.astype(jnp.bfloat16), values[...], preferred_element_type=jnp.float32
        )
        outs.append(jnp.where(mask, mixed / total, 0.0))
    attended = functools.reduce(lambda a, b: a + b, outs).astype(jnp.bfloat16)
    state = tokens_ref[...] + jnp.dot(
        attended, wout_ref[...], preferred_element_type=jnp.float32
    )
    state_ref[...] = state.astype(jnp.bfloat16)
    class_in = layer_norm(state).astype(jnp.bfloat16)
    logits = jnp.dot(class_in, wclass_ref[...], preferred_element_type=jnp.float32)
    top = jnp.max(logits, axis=1, keepdims=True)
    log_total = top + jnp.log(jnp.sum(jnp.exp(logits - top), axis=1, keepdims=True))
    number = lax.broadcasted_iota(jnp.int32, logits.shape, 1)
    label = to_column(labels_ref[...], here)
    picked = jnp.sum(jnp.where(number == label, logits, 0.0), axis=1, keepdims=True)
    loss = jnp.broadcast_to(log_total - picked, (here, here))
    same = lax.broadcasted_iota(jnp.int32, (here, here), 0) == lax.broadcasted_iota(
        jnp.int32, (here, here), 1
    )
    loss_ref[...] = jnp.sum(jnp.where(same, loss, 0.0), axis=0, keepdims=True)


VM = pl.BlockSpec(memory_space=pltpu.VMEM)


def params():
    return pltpu.CompilerParams(vmem_limit_bytes=VMEM_LIMIT)


def xor_permute(x, axis, mask, count):
    return lax.ppermute(x, axis, [(i, i ^ mask) for i in range(count)])


def gather_blocks(x):
    for axis in AXES:
        count = lax.axis_size(axis)
        bits = count.bit_length() - 1
        while bits > 0:
            low = max(bits - 2, 0)
            masks = [m << low for m in range(1, 1 << (bits - low))]
            x = jnp.concatenate([x] + [xor_permute(x, axis, m, count) for m in masks], axis=0)
            bits = low
    return x


def local(
    pixels, dw_kernel, dw_bias, norm_gain, w_expand, w_reduce, layer_scale, pixel_slot,
    intersection, parcel_pos, parcel_embed, attn_gain, w_qkv, w_out, w_class, labels,
):
    scenes, rows, width, chans = pixels.shape
    ksz = dw_kernel.shape[0]
    reach = ksz // 2
    slots = intersection.shape[1]
    owners = lax.axis_size("space") * lax.axis_size("scene")
    count = lax.axis_size("space")
    up = [(i, i + 1) for i in range(count - 1)]
    down = [(i + 1, i) for i in range(count - 1)]
    top = lax.ppermute(pixels[:, rows - reach :], "space", up)
    bottom = lax.ppermute(pixels[:, :reach], "space", down)

    taps = dw_kernel.reshape(ksz * ksz, chans)
    bias = dw_bias.reshape(1, chans)
    gain = norm_gain.reshape(1, chans)
    scale = layer_scale.reshape(1, chans)
    slab = pltpu.VMEM((chans // LANES, BLOCK_ROWS + ksz - 1, width + 2 * MARGIN, LANES), jnp.float32)
    spat = pltpu.VMEM((BLOCK_ROWS * width, chans), jnp.float32)
    wb = pltpu.VMEM((chans // LANES, ksz * ksz, 8, LANES), jnp.float32)
    work = 2 * rows * width * chans * (ksz * ksz + 2 * w_expand.shape[1])
    feats, sums, counts = pl.pallas_call(
        functools.partial(inner_kernel, rows, slots),
        grid=(scenes,),
        out_shape=(
            jax.ShapeDtypeStruct(pixels.shape, jnp.bfloat16),
            jax.ShapeDtypeStruct((slots, chans), jnp.float32),
            jax.ShapeDtypeStruct((slots, LANES), jnp.float32),
        ),
        in_specs=[VM] * 8,
        out_specs=(VM, VM, VM),
        scratch_shapes=[slab, spat, wb],
        compiler_params=params(),
        cost_estimate=pl.CostEstimate(flops=work, bytes_accessed=6 << 20, transcendentals=0),
        name="inner_rows",
    )(pixels, pixel_slot, taps, bias, gain, w_expand, w_reduce, scale)
    features, sent = pl.pallas_call(
        functools.partial(edge_kernel, rows, slots, owners),
        grid=(scenes,),
        out_shape=(
            jax.ShapeDtypeStruct(pixels.shape, jnp.bfloat16),
            jax.ShapeDtypeStruct((owners, CAP * chans + LANES), jnp.float32),
        ),
        in_specs=[VM] * 15,
        out_specs=(VM, VM),
        scratch_shapes=[
            slab, spat, wb,
            pltpu.VMEM((slots, chans), jnp.float32),
            pltpu.VMEM((slots, LANES), jnp.float32),
        ],
        compiler_params=params(),
        cost_estimate=pl.CostEstimate(flops=work, bytes_accessed=6 << 20, transcendentals=0),
        name="edge_rows",
    )(
        pixels, top, bottom, pixel_slot, taps, bias, gain, w_expand, w_reduce, scale,
        feats, sums, counts, intersection, parcel_pos.reshape(1, -1),
    )
    wide = sent.shape[1]
    arrived = lax.all_to_all(
        sent.reshape(owners, 1, wide), AXES, split_axis=0, concat_axis=0, tiled=True
    ).reshape(owners, wide)
    tokens, attn_in = pl.pallas_call(
        owner_kernel,
        out_shape=(
            jax.ShapeDtypeStruct((PAR_DEV, chans), jnp.float32),
            jax.ShapeDtypeStruct((PAR_DEV, chans), jnp.bfloat16),
        ),
        in_specs=[VM] * 3,
        out_specs=(VM, VM),
        compiler_params=params(),
        name="own_tokens",
    )(arrived, parcel_embed, attn_gain.reshape(1, chans))
    everyone = gather_blocks(attn_in)
    parcels = everyone.shape[0]
    state, loss = pl.pallas_call(
        attend_kernel,
        out_shape=(
            jax.ShapeDtypeStruct((PAR_DEV, chans), jnp.bfloat16),
            jax.ShapeDtypeStruct((1, PAR_DEV), jnp.float32),
        ),
        in_specs=[VM] * 7,
        out_specs=(VM, VM),
        scratch_shapes=[
            pltpu.VMEM((parcels, chans), jnp.bfloat16),
            pltpu.VMEM((parcels, chans), jnp.bfloat16),
        ],
        compiler_params=params(),
        name="attend",
    )(tokens, attn_in, everyone, w_qkv, w_out, w_class, labels.reshape(1, -1))
    return features, state, loss.reshape(-1)


def solution(mesh):
    in_specs = (
        P("scene", "space", None, None),
        P(), P(), P(), P(), P(), P(),
        P("scene", "space", None),
        P(AXES, None),
        P(),
        P(AXES, None),
        P(), P(), P(), P(),
        P(AXES),
    )
    out_specs = (P("scene", "space", None, None), P(AXES, None), P(AXES))
    return jax.shard_map(local, mesh=mesh, in_specs=in_specs, out_specs=out_specs, check_vma=False)
```

```python
import functools

import jax
import jax.numpy as jnp
from jax import lax
from jax.experimental import pallas as pl
from jax.experimental.pallas import tpu as pltpu
from jax.sharding import PartitionSpec as P

CAP = 3
PAR_DEV = 64
HEADS = 6
HEAD_DIM = 64
BLOCK_ROWS = 4
MARGIN = 8
LANES = 128
EPS = 1e-06
HID_CHUNK = 512
TILE_COLS = 32
TAP_ROWS = 16
ROUTE = 1 << 34
AXES = ("space", "scene")
HIGHEST = lax.Precision.HIGHEST

def gelu(x):
    half = 0.5 * x
    return half + half * lax.erf(x * 0.5**0.5)


def layer_norm(values):
    average = jnp.mean(values, axis=-1, keepdims=True)
    centered = values - average
    return centered * lax.rsqrt(jnp.mean(centered * centered, axis=-1, keepdims=True) + EPS)


def to_column(row, rows):
    n = row.shape[1]
    same = lax.broadcasted_iota(jnp.int32, (n, n), 0) == lax.broadcasted_iota(jnp.int32, (n, n), 1)
    return jnp.sum(jnp.where(same, jnp.broadcast_to(row, (n, n)), 0), axis=1, keepdims=True)


def to_row(column):
    n = column.shape[0]
    same = lax.broadcasted_iota(jnp.int32, (n, n), 0) == lax.broadcasted_iota(jnp.int32, (n, n), 1)
    return jnp.sum(jnp.where(same, jnp.broadcast_to(column, (n, n)), 0), axis=0, keepdims=True)


def conv_rows(source, slab, spat, base, wb, bias_ref, width):
    chans = spat.shape[1]
    ksz = dw_size(wb)
    reach = ksz // 2
    many = len(source) - ksz + 1
    for i, row in enumerate(source):
        value = row().astype(jnp.float32)
        for cb in range(chans // LANES):
            slab[cb, i, MARGIN : MARGIN + width, :] = value[:, cb * LANES : (cb + 1) * LANES]
    for cb in range(chans // LANES):
        lane = slice(cb * LANES, (cb + 1) * LANES)
        bias = bias_ref[...].reshape(1, chans)[:, lane]
        for col in range(0, width, TILE_COLS):
            parts = range(0, TILE_COLS, TAP_ROWS)
            total = [[None for _ in parts] for _ in range(many)]
            for i in range(len(source)):
                start = MARGIN - reach + col
                window = [
                    [
                        slab[cb, i, start + b + p : start + b + p + TAP_ROWS, :].astype(jnp.bfloat16)
                        for b in range(ksz)
                    ]
                    for p in parts
                ]
                for a in range(ksz):
                    r = i - a
                    if not 0 <= r < many:
                        continue
                    taps = [wb[cb, a * ksz + b] for b in range(ksz)]
                    for n in range(len(window)):
                        terms = [v * t for v, t in zip(window[n], taps)]
                        while len(terms) > 1:
                            terms = [sum(terms[k : k + 2][1:], terms[k]) for k in range(0, len(terms), 2)]
                        term = terms[0].astype(jnp.float32)
                        total[r][n] = term if total[r][n] is None else total[r][n] + term
            for r in range(many):
                for n, p in enumerate(parts):
                    at = base + r * width + col + p
                    spat[at : at + TAP_ROWS, lane] = total[r][n] + bias


def dw_size(wb):
    return int(wb.shape[1] ** 0.5 + 0.5)


def mlp_rows(spat, normed, branch, gain_ref, we_ref, wr_ref):
    normed[...] = (layer_norm(spat[...]) * gain_ref[...].reshape(1, -1)).astype(jnp.bfloat16)
    hid = we_ref.shape[1]
    chunk = min(HID_CHUNK, hid)
    for start in range(0, hid, chunk):
        pre = jnp.dot(
            normed[...], we_ref[:, start : start + chunk], preferred_element_type=jnp.float32
        )
        part = jnp.dot(
            gelu(pre).astype(jnp.bfloat16),
            wr_ref[start : start + chunk, :],
            preferred_element_type=jnp.float32,
        )
        if start == 0:
            branch[...] = part
        else:
            branch[...] += part


def prepare(slab, wb, dwk_ref, width):
    edge = jnp.zeros(slab.shape[:2] + (MARGIN, LANES), jnp.float32)
    slab[:, :, 0:MARGIN, :] = edge
    slab[:, :, MARGIN + width :, :] = edge
    ksz = dwk_ref.shape[0]
    for a in range(ksz):
        kernel = dwk_ref[a].astype(jnp.float32)
        for cb in range(wb.shape[0]):
            for b in range(ksz):
                wb[cb, a * ksz + b] = jnp.broadcast_to(
                    kernel[b : b + 1, cb * LANES : (cb + 1) * LANES], (TAP_ROWS, LANES)
                ).astype(jnp.bfloat16)


def pool(member, feats, sums_ref, counts_ref):
    sums_ref[...] += jnp.dot(member, feats, preferred_element_type=jnp.float32)
    ones = jnp.ones((member.shape[1], LANES), jnp.bfloat16)
    counts_ref[...] += jnp.dot(member, ones, preferred_element_type=jnp.float32)


def membership(slot_ref, scene, row0, many, width, slots):
    pieces = []
    for r in range(many):
        one = slot_ref[scene, row0 + r : row0 + r + 1, :]
        index = lax.broadcasted_iota(jnp.int32, (slots, width), 0)
        pieces.append((index == one).astype(jnp.float32).astype(jnp.bfloat16))
    return jnp.concatenate(pieces, axis=1)


def rows_block(
    scenes, blocks, slots, width, x_ref, slot_ref, slab, spat, normed, branch, wb, bias_ref,
    gain_ref, we_ref, wr_ref, scale_ref, feat_ref, sums_ref, counts_ref, before_mlp, after_scene,
):
    for scene in range(scenes):
        base = 0
        for _, many, window in blocks:
            conv_rows(window(scene), slab, spat, base, wb, bias_ref, width)
            base += many * width
        if scene == 0:
            before_mlp()
        mlp_rows(spat, normed, branch, gain_ref, we_ref, wr_ref)
        center = jnp.concatenate(
            [x_ref[scene, r : r + n].reshape(n * width, -1) for r, n, _ in blocks], axis=0
        )
        feats = (
            center.astype(jnp.float32) + scale_ref[...].reshape(1, -1) * branch[...]
        ).astype(jnp.bfloat16)
        feat_ref[scene] = feats
        after_scene(scene)
        member = jnp.concatenate(
            [membership(slot_ref, scene, r, n, width, slots) for r, n, _ in blocks], axis=1
        )
        pool(member, feats, sums_ref, counts_ref)


def route_kernel(owners, inter_ref, pos_ref, placer_ref, rows_ref):
    slots = inter_ref.shape[1]
    parcels = pos_ref.shape[0]
    listed = to_column(inter_ref[...], slots)
    number = lax.broadcasted_iota(jnp.int32, (slots, parcels), 1)
    position = jnp.sum(
        jnp.where(number == listed, jnp.broadcast_to(pos_ref[...].reshape(1, parcels), (slots, parcels)), 0),
        axis=1, keepdims=True,
    )
    owner = position // PAR_DEV
    owner_row = to_row(owner)
    this = lax.broadcasted_iota(jnp.int32, (slots, slots), 0)
    other = lax.broadcasted_iota(jnp.int32, (slots, slots), 1)
    rank = jnp.sum(
        jnp.where((owner == owner_row) & (other < this), 1, 0), axis=1, keepdims=True
    )
    place = to_row(rank * owners + owner)
    place_index = lax.broadcasted_iota(jnp.int32, (CAP * owners, slots), 0)
    placer_ref[...] = (place_index == place).astype(jnp.float32)
    local_row = (position - owner * PAR_DEV).astype(jnp.float32)
    rows_ref[...] = jnp.broadcast_to(local_row, rows_ref.shape)


def inner_kernel(
    rows, slots, x_hbm, slot_hbm, dwk_hbm, bias_hbm, gain_hbm, we_hbm, wr_hbm, scale_hbm,
    feat_hbm, sums_ref, counts_ref, x_ref, slot_ref, dwk_ref, bias_ref, gain_ref, we_ref, wr_ref,
    scale_ref, sems, out_sems, slab, spat, normed, branch, wb, feat_ref,
):
    scenes, _, width, _ = x_ref.shape
    ksz = dw_size(wb)
    reach = ksz // 2
    inside = rows - 2 * BLOCK_ROWS
    first = [(x_hbm, x_ref), (dwk_hbm, dwk_ref), (bias_hbm, bias_ref)]
    later = [
        (slot_hbm, slot_ref), (gain_hbm, gain_ref), (we_hbm, we_ref), (wr_hbm, wr_ref),
        (scale_hbm, scale_ref),
    ]
    copies = [pltpu.make_async_copy(a, b, sems.at[i]) for i, (a, b) in enumerate(first + later)]
    for copy in copies:
        copy.start()
    sums_ref[...] = jnp.zeros_like(sums_ref)
    counts_ref[...] = jnp.zeros_like(counts_ref)
    for copy in copies[: len(first)]:
        copy.wait()
    prepare(slab, wb, dwk_ref, width)

    def window(scene):
        return [
            functools.partial(lambda r: x_ref[scene, r], BLOCK_ROWS - reach + i)
            for i in range(inside + ksz - 1)
        ]

    def arrive():
        for copy in copies[len(first) :]:
            copy.wait()

    writes = [
        pltpu.make_async_copy(
            feat_ref.at[scene, pl.ds(r * width, width)],
            feat_hbm.at[scene, BLOCK_ROWS + r],
            out_sems.at[scene, r],
        )
        for scene in range(scenes)
        for r in range(inside)
    ]

    def leave(scene):
        for write in writes[scene * inside : (scene + 1) * inside]:
            write.start()

    rows_block(
        scenes, [(BLOCK_ROWS, inside, window)], slots, width, x_ref, slot_ref, slab, spat, normed,
        branch, wb, bias_ref, gain_ref, we_ref, wr_ref, scale_ref, feat_ref, sums_ref, counts_ref,
        arrive, leave,
    )
    for write in writes:
        write.wait()


def edge_kernel(
    rows, slots, owners, x_ref, top_ref, bot_ref, slot_ref, dwk_ref, bias_ref, gain_ref, we_ref,
    wr_ref, scale_ref, feat_in, sums_in, counts_in, placer_ref, rows_ref,
    feat_hbm, sent_ref, out_sems, slab, spat, normed, branch, wb, feat_ref, sums_ref, counts_ref,
):
    scenes, _, width, _ = x_ref.shape
    ksz = dw_size(wb)
    reach = ksz // 2
    prepare(slab, wb, dwk_ref, width)
    sums_ref[...] = sums_in[...]
    counts_ref[...] = counts_in[...]

    def window(row0):
        def rows_of(scene):
            source = []
            for i in range(BLOCK_ROWS + ksz - 1):
                r = row0 - reach + i
                if r < 0:
                    source.append(functools.partial(lambda r: top_ref[scene, r], r + reach))
                elif r >= rows:
                    source.append(functools.partial(lambda r: bot_ref[scene, r], r - rows))
                else:
                    source.append(functools.partial(lambda r: x_ref[scene, r], r))
            return source

        return rows_of

    starts = (0, rows - BLOCK_ROWS)
    writes = [
        pltpu.make_async_copy(
            feat_ref.at[scene, pl.ds((n * BLOCK_ROWS + r) * width, width)],
            feat_hbm.at[scene, start + r],
            out_sems.at[scene, n * BLOCK_ROWS + r],
        )
        for scene in range(scenes)
        for n, start in enumerate(starts)
        for r in range(BLOCK_ROWS)
    ]
    each = len(starts) * BLOCK_ROWS

    def leave(scene):
        for write in writes[scene * each : (scene + 1) * each]:
            write.start()

    rows_block(
        scenes, [(start, BLOCK_ROWS, window(start)) for start in starts], slots, width, x_ref,
        slot_ref, slab, spat, normed, branch, wb, bias_ref, gain_ref, we_ref, wr_ref, scale_ref,
        feat_ref, sums_ref, counts_ref, lambda: None, leave,
    )
    placer = placer_ref[...]
    sent = jnp.dot(placer, sums_ref[...], precision=HIGHEST, preferred_element_type=jnp.float32)
    lane = lax.broadcasted_iota(jnp.int32, (slots, LANES), 1)
    counts_rows = jnp.where(lane < CAP, counts_ref[...], rows_ref[...])
    meta = jnp.dot(placer, counts_rows, precision=HIGHEST, preferred_element_type=jnp.float32)
    chans = sent.shape[1]
    lane = lax.broadcasted_iota(jnp.int32, (owners, LANES), 1)
    packed = jnp.zeros((owners, LANES), jnp.float32)
    for k in range(CAP):
        sent_ref[:, 0, k * chans : (k + 1) * chans] = sent[k * owners : (k + 1) * owners]
        packed = jnp.where(
            (lane == k) | (lane == CAP + k), meta[k * owners : (k + 1) * owners], packed
        )
    sent_ref[:, 0, CAP * chans :] = packed
    for write in writes:
        write.wait()


def owner_kernel(recv_ref, embed_ref, gain_ref, tokens_ref, attn_ref):
    chans = embed_ref.shape[1]
    meta = recv_ref[:, 0, CAP * chans :]
    tiles = recv_ref.shape[0]
    sums = jnp.zeros(tokens_ref.shape, jnp.float32)
    counts = jnp.zeros((PAR_DEV, LANES), jnp.float32)
    index = lax.broadcasted_iota(jnp.int32, (PAR_DEV, tiles), 0).astype(jnp.float32)
    for k in range(CAP):
        rows = jnp.broadcast_to(meta[:, CAP + k : CAP + k + 1], (tiles, LANES)).T[0:1, :]
        table = (index == rows).astype(jnp.float32)
        sums += jnp.dot(
            table, recv_ref[:, 0, k * chans : (k + 1) * chans],
            precision=HIGHEST, preferred_element_type=jnp.float32,
        )
        many = jnp.broadcast_to(meta[:, k : k + 1], (tiles, LANES))
        counts += jnp.dot(table, many, precision=HIGHEST, preferred_element_type=jnp.float32)
    tokens = sums / jnp.maximum(counts[:, :1], 1.0) + embed_ref[...].astype(jnp.float32)
    tokens_ref[...] = tokens
    attn_ref[...] = (layer_norm(tokens) * gain_ref[...].reshape(1, chans)).astype(jnp.bfloat16)


def fold_keys(pieces, queries, wqkv_ref, state):
    chans = wqkv_ref.shape[0]
    part = jnp.concatenate([p[...] for p in pieces], axis=0)
    keys = jnp.dot(
        part, wqkv_ref[:, chans : 2 * chans], preferred_element_type=jnp.float32
    ).astype(jnp.bfloat16)
    values = jnp.dot(
        part, wqkv_ref[:, 2 * chans :], preferred_element_type=jnp.float32
    ).astype(jnp.bfloat16)
    scores = lax.dot_general(
        queries, keys, (((1,), (1,)), ((), ())), preferred_element_type=jnp.float32
    )
    top = jnp.max(scores, axis=1, keepdims=True)
    if state is not None:
        top = jnp.maximum(state[0], top)
    weights = jnp.exp(scores - top)
    total = jnp.sum(weights, axis=1, keepdims=True)
    mixed = jnp.dot(weights.astype(jnp.bfloat16), values, preferred_element_type=jnp.float32)
    if state is not None:
        keep = jnp.exp(state[0] - top)
        total = total + keep * state[1]
        mixed = mixed + keep * state[2]
    return top, total, mixed


def split_heads(own_ref, wqkv_ref):
    chans = wqkv_ref.shape[0]
    queries = jnp.dot(
        own_ref[...], wqkv_ref[:, :chans], preferred_element_type=jnp.float32
    ) * HEAD_DIM ** (-0.5)
    lane = lax.broadcasted_iota(jnp.int32, queries.shape, 1)
    return jnp.concatenate(
        [jnp.where(lane // HEAD_DIM == h, queries, 0.0).astype(jnp.bfloat16) for h in range(HEADS)],
        axis=0,
    )


def near_kernel(count, own_ref, wqkv_ref, *refs):
    pieces, (stat_ref, mixed_ref, query_ref) = refs[:count], refs[count:]
    queries = split_heads(own_ref, wqkv_ref)
    query_ref[...] = queries
    top, total, mixed = fold_keys(pieces, queries, wqkv_ref, None)
    lane = lax.broadcasted_iota(jnp.int32, stat_ref.shape, 1)
    stat_ref[...] = jnp.where(lane == 0, top, total)
    mixed_ref[...] = mixed


def far_kernel(
    count, tokens_ref, query_ref, wqkv_ref, wout_ref, wclass_ref, labels_ref, stat_ref, mixed_ref,
    *refs,
):
    pieces, (state_ref, loss_ref) = refs[:count], refs[count:]
    chans = wqkv_ref.shape[0]
    here = tokens_ref.shape[0]
    state = (stat_ref[:, 0:1], stat_ref[:, 1:2], mixed_ref[...])
    _, total, mixed = fold_keys(pieces, query_ref[...], wqkv_ref, state)
    mixed = mixed / total
    lane = lax.broadcasted_iota(jnp.int32, (here, chans), 1)
    attended = jnp.zeros((here, chans), jnp.float32)
    for h in range(HEADS):
        attended = jnp.where(lane // HEAD_DIM == h, mixed[h * here : (h + 1) * here], attended)
    state = tokens_ref[...] + jnp.dot(
        attended.astype(jnp.bfloat16), wout_ref[...], preferred_element_type=jnp.float32
    )
    state_ref[...] = state.astype(jnp.bfloat16)
    class_in = layer_norm(state).astype(jnp.bfloat16)
    logits = lax.dot_general(
        class_in, wclass_ref[...], (((1,), (1,)), ((), ())), preferred_element_type=jnp.float32
    )
    top = jnp.max(logits, axis=1, keepdims=True)
    log_total = top + jnp.log(jnp.sum(jnp.exp(logits - top), axis=1, keepdims=True))
    number = lax.broadcasted_iota(jnp.int32, logits.shape, 1)
    label = to_column(labels_ref[...].reshape(1, here), here)
    picked = jnp.sum(jnp.where(number == label, logits, 0.0), axis=1, keepdims=True)
    loss = jnp.broadcast_to(log_total - picked, (here, here))
    same = lax.broadcasted_iota(jnp.int32, (here, here), 0) == lax.broadcasted_iota(
        jnp.int32, (here, here), 1
    )
    loss_ref[...] = jnp.sum(jnp.where(same, loss, 0.0), axis=0)


VM = pl.BlockSpec(memory_space=pltpu.VMEM)
HBM = pl.BlockSpec(memory_space=pltpu.HBM)


def params(mib=32):
    return pltpu.CompilerParams(vmem_limit_bytes=mib * 1024 * 1024)


def xor_permute(x, axis, mask, count):
    return lax.ppermute(x, axis, [(i, i ^ mask) for i in range(count)])


def exchange(groups, axis, bits, count):
    whole = groups[0] if len(groups) == 1 else jnp.concatenate(groups, axis=0)
    masks = [sum(1 << b for n, b in enumerate(bits) if m >> n & 1) for m in range(1, 1 << len(bits))]
    return [whole], [xor_permute(whole, axis, m, count) for m in masks]


def gather_stages():
    stages = []
    for axis in AXES:
        bits = list(range(lax.axis_size(axis).bit_length() - 1))[::-1]
        last = [bits.pop()] if axis == AXES[-1] else []
        stages += [(axis, bits[i : i + 2]) for i in range(0, len(bits), 2)]
        if last:
            stages.append((axis, last))
    return stages


def local(
    pixels, dw_kernel, dw_bias, norm_gain, w_expand, w_reduce, layer_scale, pixel_slot,
    intersection, parcel_pos, parcel_embed, attn_gain, w_qkv, w_out, w_class, labels,
):
    scenes, rows, width, chans = pixels.shape
    ksz = dw_kernel.shape[0]
    reach = ksz // 2
    slots = intersection.shape[1]
    owners = lax.axis_size("space") * lax.axis_size("scene")
    count = lax.axis_size("space")
    up = [(i, i + 1) for i in range(count - 1)]
    down = [(i + 1, i) for i in range(count - 1)]
    top = lax.ppermute(pixels[:, rows - reach :], "space", up)
    bottom = lax.ppermute(pixels[:, :reach], "space", down)

    inside = rows - 2 * BLOCK_ROWS

    def scratch(many, window):
        return [
            pltpu.SemaphoreType.DMA((scenes, many)),
            pltpu.VMEM((chans // LANES, window, width + 2 * MARGIN, LANES), jnp.float32),
            pltpu.VMEM((many * width, chans), jnp.float32),
            pltpu.VMEM((many * width, chans), jnp.bfloat16),
            pltpu.VMEM((many * width, chans), jnp.float32),
            pltpu.VMEM((chans // LANES, ksz * ksz, TAP_ROWS, LANES), jnp.bfloat16),
            pltpu.VMEM((scenes, many * width, chans), jnp.bfloat16),
        ]

    work = 2 * rows * width * chans * (ksz * ksz + 2 * w_expand.shape[1])
    placer, local_rows = pl.pallas_call(
        functools.partial(route_kernel, owners),
        out_shape=(
            jax.ShapeDtypeStruct((CAP * owners, slots), jnp.float32),
            jax.ShapeDtypeStruct((slots, LANES), jnp.float32),
        ),
        in_specs=[VM] * 2,
        out_specs=(VM, VM),
        compiler_params=params(8),
        cost_estimate=pl.CostEstimate(flops=ROUTE, bytes_accessed=1 << 20, transcendentals=0),
        name="route",
    )(intersection, parcel_pos)
    inputs = (
        pixels, pixel_slot, dw_kernel, dw_bias, norm_gain, w_expand, w_reduce, layer_scale
    )
    feats, sums, counts = pl.pallas_call(
        functools.partial(inner_kernel, rows, slots),
        out_shape=(
            jax.ShapeDtypeStruct(pixels.shape, jnp.bfloat16),
            jax.ShapeDtypeStruct((slots, chans), jnp.float32),
            jax.ShapeDtypeStruct((slots, LANES), jnp.float32),
        ),
        in_specs=[HBM] * len(inputs),
        out_specs=(HBM, VM, VM),
        scratch_shapes=[pltpu.VMEM(v.shape, v.dtype) for v in inputs]
        + [pltpu.SemaphoreType.DMA((len(inputs),))]
        + scratch(inside, inside + ksz - 1),
        compiler_params=params(),
        cost_estimate=pl.CostEstimate(flops=work, bytes_accessed=6 << 20, transcendentals=0),
        name="inner_rows",
    )(*inputs)
    features, sent = pl.pallas_call(
        functools.partial(edge_kernel, rows, slots, owners),
        out_shape=(
            jax.ShapeDtypeStruct(pixels.shape, jnp.bfloat16),
            jax.ShapeDtypeStruct((owners, 1, CAP * chans + LANES), jnp.float32),
        ),
        in_specs=[VM] * 10 + [HBM] + [VM] * 4,
        out_specs=(HBM, VM),
        input_output_aliases={10: 0},
        scratch_shapes=scratch(2 * BLOCK_ROWS, BLOCK_ROWS + ksz - 1)
        + [pltpu.VMEM((slots, chans), jnp.float32), pltpu.VMEM((slots, LANES), jnp.float32)],
        compiler_params=params(),
        cost_estimate=pl.CostEstimate(flops=work, bytes_accessed=6 << 20, transcendentals=0),
        name="edge_rows",
    )(
        pixels, top, bottom, pixel_slot, dw_kernel, dw_bias, norm_gain, w_expand, w_reduce, layer_scale,
        feats, sums, counts, placer, local_rows,
    )
    arrived = lax.all_to_all(sent, AXES, split_axis=0, concat_axis=0, tiled=True)
    tokens, attn_in = pl.pallas_call(
        owner_kernel,
        out_shape=(
            jax.ShapeDtypeStruct((PAR_DEV, chans), jnp.float32),
            jax.ShapeDtypeStruct((PAR_DEV, chans), jnp.bfloat16),
        ),
        in_specs=[VM] * 3,
        out_specs=(VM, VM),
        compiler_params=params(),
        name="own_tokens",
    )(arrived, parcel_embed, attn_gain)
    held = [attn_in]
    stages = gather_stages()
    for axis, bits in stages[:-1]:
        kept, got = exchange(held, axis, bits, lax.axis_size(axis))
        held = kept + got
    axis, bits = stages[-1]
    far = [xor_permute(h, axis, 1 << bits[0], lax.axis_size(axis)) for h in held]
    heads = HEADS * PAR_DEV
    fold = 2 * owners * PAR_DEV * chans * (chans + heads)
    stat, mixed, queries = pl.pallas_call(
        functools.partial(near_kernel, len(held)),
        out_shape=(
            jax.ShapeDtypeStruct((heads, LANES), jnp.float32),
            jax.ShapeDtypeStruct((heads, chans), jnp.float32),
            jax.ShapeDtypeStruct((heads, chans), jnp.bfloat16),
        ),
        in_specs=[VM] * (2 + len(held)),
        out_specs=(VM,) * 3,
        compiler_params=params(),
        cost_estimate=pl.CostEstimate(flops=fold, bytes_accessed=2 << 20, transcendentals=0),
        name="near_keys",
    )(attn_in, w_qkv, *held)
    state, loss = pl.pallas_call(
        functools.partial(far_kernel, len(far)),
        out_shape=(
            jax.ShapeDtypeStruct((PAR_DEV, chans), jnp.bfloat16),
            jax.ShapeDtypeStruct((PAR_DEV,), jnp.float32),
        ),
        in_specs=[VM] * (8 + len(far)),
        out_specs=(VM, VM),
        compiler_params=params(),
        cost_estimate=pl.CostEstimate(flops=fold, bytes_accessed=2 << 20, transcendentals=0),
        name="far_keys",
    )(tokens, queries, w_qkv, w_out, w_class.T, labels, stat, mixed, *far)
    return features, state, loss


def solution(mesh):
    in_specs = (
        P("scene", "space", None, None),
        P(), P(), P(), P(), P(), P(),
        P("scene", "space", None),
        P(AXES, None),
        P(),
        P(AXES, None),
        P(), P(), P(), P(),
        P(AXES),
    )
    out_specs = (P("scene", "space", None, None), P(AXES, None), P(AXES))
    return jax.shard_map(local, mesh=mesh, in_specs=in_specs, out_specs=out_specs, check_vma=False)
```

```python
import functools

import jax
import jax.numpy as jnp
from jax import lax
from jax.experimental import pallas as pl
from jax.experimental.pallas import tpu as pltpu
from jax.sharding import PartitionSpec as P

CAP = 3
PAR_DEV = 64
HEADS = 6
HEAD_DIM = 64
BLOCK_ROWS = 4
MARGIN = 8
LANES = 128
EPS = 1e-06
TILE_COLS = 32
PIECE = 512
TAP_ROWS = 16
START = 1 << 34
AXES = ("space", "scene")
HIGHEST = lax.Precision.HIGHEST

def gelu(x):
    half = 0.5 * x
    return half + half * lax.erf(x * 0.5**0.5)


def layer_norm(values):
    average = jnp.mean(values, axis=-1, keepdims=True)
    centered = values - average
    return centered * lax.rsqrt(jnp.mean(centered * centered, axis=-1, keepdims=True) + EPS)


def to_column(row, rows):
    n = row.shape[1]
    same = lax.broadcasted_iota(jnp.int32, (n, n), 0) == lax.broadcasted_iota(jnp.int32, (n, n), 1)
    return jnp.sum(jnp.where(same, jnp.broadcast_to(row, (n, n)), 0), axis=1, keepdims=True)


def to_row(column):
    n = column.shape[0]
    same = lax.broadcasted_iota(jnp.int32, (n, n), 0) == lax.broadcasted_iota(jnp.int32, (n, n), 1)
    return jnp.sum(jnp.where(same, jnp.broadcast_to(column, (n, n)), 0), axis=0, keepdims=True)


def fill(windows, slab, width):
    for n, window in enumerate(windows):
        for i, row in enumerate(window):
            value = row().astype(jnp.float32)
            for cb in range(slab.shape[1]):
                slab[n, cb, i, MARGIN : MARGIN + width, :] = value[:, cb * LANES : (cb + 1) * LANES]


def conv_tile(n, cb, col, slab, spat, wb, bias_ref, width):
    ksz = dw_size(wb)
    start = MARGIN - ksz // 2 + col
    parts = range(0, TILE_COLS, TAP_ROWS)
    total = [[None for _ in parts] for _ in range(BLOCK_ROWS)]
    for i in range(slab.shape[2]):
        window = [
            [
                slab[n, cb, i, start + b + p : start + b + p + TAP_ROWS, :].astype(jnp.bfloat16)
                for b in range(ksz)
            ]
            for p in parts
        ]
        for a in range(ksz):
            r = i - a
            if not 0 <= r < BLOCK_ROWS:
                continue
            taps = [wb[cb, a * ksz + b] for b in range(ksz)]
            for k in range(len(window)):
                terms = [v * t for v, t in zip(window[k], taps)]
                while len(terms) > 1:
                    terms = [sum(terms[j + 1 : j + 2], terms[j]) for j in range(0, len(terms), 2)]
                term = terms[0].astype(jnp.float32)
                total[r][k] = term if total[r][k] is None else total[r][k] + term
    bias = bias_ref[cb, 0:1, :]
    for r in range(BLOCK_ROWS):
        for k, p in enumerate(parts):
            at = (n * BLOCK_ROWS + r) * width + col + p
            spat[cb, pl.ds(at, TAP_ROWS), :] = total[r][k] + bias


def dw_size(wb):
    return int(wb.shape[1] ** 0.5 + 0.5)


def norm_rows(spat, normed, gain_ref):
    values = jnp.concatenate([spat[cb] for cb in range(spat.shape[0])], axis=1)
    normed[...] = (layer_norm(values) * gain_ref[...].reshape(1, -1)).astype(jnp.bfloat16)


def rows_step(
    convolve, pointwise, slab, spat, normed, branch, ahead, wb, bias_ref, we_ref, wr_ref, width
):
    blocks, chan_blocks = slab.shape[:2]
    steps = blocks * chan_blocks
    chunk = we_ref.shape[1] // steps
    many = normed.shape[0]
    cols = list(range(0, width, TILE_COLS))

    def expand(part, slot, r):
        at = part * chunk
        ahead[slot, r : r + PIECE] = jnp.dot(
            normed[r : r + PIECE], we_ref[:, pl.ds(at, chunk)], preferred_element_type=jnp.float32
        )

    def reduce(part, slot, r):
        at = part * chunk
        branch[r : r + PIECE] += jnp.dot(
            gelu(ahead[slot, r : r + PIECE]).astype(jnp.bfloat16),
            wr_ref[pl.ds(at, chunk), :],
            preferred_element_type=jnp.float32,
        )

    def step(cb, carry):
        for n in range(blocks):
            part = cb * blocks + n
            todo = list(cols) if convolve else []
            for r in range(0, many, PIECE):
                if pointwise:
                    expand(min(part + 1, steps - 1), (n + 1) % blocks, r)
                    reduce(part, n, r)
                if todo:
                    conv_tile(n, cb, todo.pop(0), slab, spat, wb, bias_ref, width)
            for col in todo:
                conv_tile(n, cb, col, slab, spat, wb, bias_ref, width)
        return carry

    if pointwise:
        branch[...] = jnp.zeros_like(branch)
        for r in range(0, many, PIECE):
            expand(0, 0, r)
    for cb in range(chan_blocks):
        step(cb, 0)


def prepare(slab, wb, bias, dwk_ref, bias_ref, width):
    edge = jnp.zeros(slab.shape[:3] + (MARGIN, LANES), jnp.float32)
    slab[:, :, :, 0:MARGIN, :] = edge
    slab[:, :, :, MARGIN + width :, :] = edge
    values = bias_ref[...].reshape(1, -1)
    for cb in range(wb.shape[0]):
        bias[cb] = jnp.broadcast_to(values[:, cb * LANES : (cb + 1) * LANES], (8, LANES))
    ksz = dwk_ref.shape[0]
    for a in range(ksz):
        kernel = dwk_ref[a].astype(jnp.float32)
        for cb in range(wb.shape[0]):
            for b in range(ksz):
                wb[cb, a * ksz + b] = jnp.broadcast_to(
                    kernel[b : b + 1, cb * LANES : (cb + 1) * LANES], (TAP_ROWS, LANES)
                ).astype(jnp.bfloat16)


def pool(member, feats, sums_ref, counts_ref):
    sums_ref[...] += jnp.dot(member, feats, preferred_element_type=jnp.float32)
    ones = jnp.ones((member.shape[1], LANES), jnp.bfloat16)
    counts_ref[...] += jnp.dot(member, ones, preferred_element_type=jnp.float32)


def membership(slot_ref, scene, row0, many, width, slots):
    pieces = []
    for r in range(many):
        one = slot_ref[scene, row0 + r : row0 + r + 1, :]
        index = lax.broadcasted_iota(jnp.int32, (slots, width), 0)
        pieces.append((index == one).astype(jnp.float32).astype(jnp.bfloat16))
    return jnp.concatenate(pieces, axis=1)


def finish_rows(
    scene, starts, n, slots, width, x_ref, slot_ref, branch, scale_ref, feat_ref, sums_ref,
    counts_ref, feat_hbm, out_sems,
):
    size = BLOCK_ROWS * width
    center = jnp.concatenate(
        [x_ref[scene, r : r + BLOCK_ROWS].reshape(size, -1) for r in starts], axis=0
    )
    feats = (
        center.astype(jnp.float32) + scale_ref[...].reshape(1, -1) * branch[...]
    ).astype(jnp.bfloat16)
    feat_ref[n] = feats.reshape(len(starts) * BLOCK_ROWS, width, -1)
    writes = [
        pltpu.make_async_copy(
            feat_ref.at[n, pl.ds(k * BLOCK_ROWS, BLOCK_ROWS)],
            feat_hbm.at[scene, pl.ds(r, BLOCK_ROWS)],
            out_sems.at[n, k],
        )
        for k, r in enumerate(starts)
    ]
    for write in writes:
        write.start()
    member = jnp.concatenate(
        [membership(slot_ref, scene, r, BLOCK_ROWS, width, slots) for r in starts], axis=1
    )
    pool(member, feats, sums_ref, counts_ref)
    return writes


def window_rows(scene, row0, reach, rows, x_ref, top_ref, bot_ref):
    source = []
    for r in range(row0 - reach, row0 + BLOCK_ROWS + reach):
        if r < 0:
            source.append(functools.partial(lambda r: top_ref[scene, r], r + reach))
        elif r >= rows:
            source.append(functools.partial(lambda r: bot_ref[scene, r], r - rows))
        else:
            source.append(functools.partial(lambda r: x_ref[scene, r], r))
    return source


def start_kernel(sums_ref, counts_ref):
    sums_ref[...] = jnp.zeros_like(sums_ref)
    counts_ref[...] = jnp.zeros_like(counts_ref)


def route(owners, inter_ref, pos_ref, placer_ref, rows_ref):
    slots = inter_ref.shape[1]
    parcels = pos_ref.shape[0]
    listed = to_column(inter_ref[...], slots)
    number = lax.broadcasted_iota(jnp.int32, (slots, parcels), 1)
    position = jnp.sum(
        jnp.where(number == listed, jnp.broadcast_to(pos_ref[...].reshape(1, parcels), (slots, parcels)), 0),
        axis=1, keepdims=True,
    )
    owner = position // PAR_DEV
    owner_row = to_row(owner)
    this = lax.broadcasted_iota(jnp.int32, (slots, slots), 0)
    other = lax.broadcasted_iota(jnp.int32, (slots, slots), 1)
    rank = jnp.sum(
        jnp.where((owner == owner_row) & (other < this), 1, 0), axis=1, keepdims=True
    )
    place = to_row(rank * owners + owner)
    place_index = lax.broadcasted_iota(jnp.int32, (CAP * owners, slots), 0)
    placer_ref[...] = (place_index == place).astype(jnp.float32)
    local_row = (position - owner * PAR_DEV).astype(jnp.float32)
    rows_ref[...] = jnp.broadcast_to(local_row, rows_ref.shape)


def inner_kernel(
    rows, slots, owners, x_ref, slot_ref, dwk_ref, bias_ref, gain_ref, we_ref, wr_ref, scale_ref,
    sums_in, counts_in, inter_ref, pos_ref,
    feat_hbm, sums_ref, counts_ref, normed, placer_ref, rows_ref, out_sems, slab, spat, branch, ahead, wb, bias, feat_ref,
):
    scenes, _, width, _ = x_ref.shape
    reach = dw_size(wb) // 2
    sums_ref[...] = sums_in[...]
    counts_ref[...] = counts_in[...]
    route(owners, inter_ref, pos_ref, placer_ref, rows_ref)
    prepare(slab, wb, bias, dwk_ref, bias_ref, width)
    starts = range(BLOCK_ROWS, rows - BLOCK_ROWS, BLOCK_ROWS)
    writes = []
    for scene in range(scenes):
        fill(
            [window_rows(scene, r, reach, rows, x_ref, None, None) for r in starts], slab, width
        )
        rows_step(
            True, scene > 0, slab, spat, normed, branch, ahead, wb, bias, we_ref, wr_ref, width
        )
        if scene > 0:
            writes += finish_rows(
                scene - 1, starts, scene - 1, slots, width, x_ref, slot_ref, branch, scale_ref,
                feat_ref, sums_ref, counts_ref, feat_hbm, out_sems,
            )
        norm_rows(spat, normed, gain_ref)
    for write in writes:
        write.wait()


def edge_kernel(
    rows, slots, owners, x_ref, top_ref, bot_ref, slot_ref, dwk_ref, bias_ref, gain_ref, we_ref,
    wr_ref, scale_ref, feat_in, sums_in, counts_in, normed_in, placer_ref, rows_ref,
    feat_hbm, sent_ref, out_sems, slab, spat, branch, ahead, wb, bias, feat_ref, normed, sums_ref,
    counts_ref,
):
    scenes, _, width, _ = x_ref.shape
    reach = dw_size(wb) // 2
    sums_ref[...] = sums_in[...]
    counts_ref[...] = counts_in[...]
    normed[...] = normed_in[...]
    prepare(slab, wb, bias, dwk_ref, bias_ref, width)
    inside = range(BLOCK_ROWS, rows - BLOCK_ROWS, BLOCK_ROWS)
    outside = (0, rows - BLOCK_ROWS)
    writes = []
    for n in range(scenes + 1):
        if n < scenes:
            fill(
                [window_rows(n, r, reach, rows, x_ref, top_ref, bot_ref) for r in outside],
                slab, width,
            )
        rows_step(
            n < scenes, True, slab, spat, normed, branch, ahead, wb, bias, we_ref, wr_ref, width
        )
        scene, starts = (scenes - 1, inside) if n == 0 else (n - 1, outside)
        writes += finish_rows(
            scene, starts, n, slots, width, x_ref, slot_ref, branch, scale_ref, feat_ref,
            sums_ref, counts_ref, feat_hbm, out_sems,
        )
        if n < scenes:
            norm_rows(spat, normed, gain_ref)
    placer = placer_ref[...]
    sent = jnp.dot(placer, sums_ref[...], precision=HIGHEST, preferred_element_type=jnp.float32)
    lane = lax.broadcasted_iota(jnp.int32, (slots, LANES), 1)
    counts_rows = jnp.where(lane < CAP, counts_ref[...], rows_ref[...])
    meta = jnp.dot(placer, counts_rows, precision=HIGHEST, preferred_element_type=jnp.float32)
    chans = sent.shape[1]
    lane = lax.broadcasted_iota(jnp.int32, (owners, LANES), 1)
    packed = jnp.zeros((owners, LANES), jnp.float32)
    for k in range(CAP):
        sent_ref[:, 0, k * chans : (k + 1) * chans] = sent[k * owners : (k + 1) * owners]
        packed = jnp.where(
            (lane == k) | (lane == CAP + k), meta[k * owners : (k + 1) * owners], packed
        )
    sent_ref[:, 0, CAP * chans :] = packed
    for write in writes:
        write.wait()


def owner_kernel(recv_ref, embed_ref, gain_ref, tokens_ref, attn_ref):
    chans = embed_ref.shape[1]
    meta = recv_ref[:, 0, CAP * chans :]
    tiles = recv_ref.shape[0]
    sums = jnp.zeros(tokens_ref.shape, jnp.float32)
    counts = jnp.zeros((PAR_DEV, LANES), jnp.float32)
    index = lax.broadcasted_iota(jnp.int32, (PAR_DEV, tiles), 0).astype(jnp.float32)
    for k in range(CAP):
        rows = jnp.broadcast_to(meta[:, CAP + k : CAP + k + 1], (tiles, LANES)).T[0:1, :]
        table = (index == rows).astype(jnp.float32)
        sums += jnp.dot(
            table, recv_ref[:, 0, k * chans : (k + 1) * chans],
            precision=HIGHEST, preferred_element_type=jnp.float32,
        )
        many = jnp.broadcast_to(meta[:, k : k + 1], (tiles, LANES))
        counts += jnp.dot(table, many, precision=HIGHEST, preferred_element_type=jnp.float32)
    tokens = sums / jnp.maximum(counts[:, :1], 1.0) + embed_ref[...].astype(jnp.float32)
    tokens_ref[...] = tokens
    attn_ref[...] = (layer_norm(tokens) * gain_ref[...].reshape(1, chans)).astype(jnp.bfloat16)


def fold_keys(pieces, queries, wqkv_ref, state):
    chans = wqkv_ref.shape[0]
    part = jnp.concatenate([p[...] for p in pieces], axis=0)
    keys = jnp.dot(
        part, wqkv_ref[:, chans : 2 * chans], preferred_element_type=jnp.float32
    ).astype(jnp.bfloat16)
    values = jnp.dot(
        part, wqkv_ref[:, 2 * chans :], preferred_element_type=jnp.float32
    ).astype(jnp.bfloat16)
    scores = lax.dot_general(
        queries, keys, (((1,), (1,)), ((), ())), preferred_element_type=jnp.float32
    )
    top = jnp.max(scores, axis=1, keepdims=True)
    if state is not None:
        top = jnp.maximum(state[0], top)
    weights = jnp.exp(scores - top)
    total = jnp.sum(weights, axis=1, keepdims=True)
    mixed = jnp.dot(weights.astype(jnp.bfloat16), values, preferred_element_type=jnp.float32)
    if state is not None:
        keep = jnp.exp(state[0] - top)
        total = total + keep * state[1]
        mixed = mixed + keep * state[2]
    return top, total, mixed


def split_heads(own_ref, wqkv_ref):
    chans = wqkv_ref.shape[0]
    queries = jnp.dot(
        own_ref[...], wqkv_ref[:, :chans], preferred_element_type=jnp.float32
    ) * HEAD_DIM ** (-0.5)
    lane = lax.broadcasted_iota(jnp.int32, queries.shape, 1)
    return jnp.concatenate(
        [jnp.where(lane // HEAD_DIM == h, queries, 0.0).astype(jnp.bfloat16) for h in range(HEADS)],
        axis=0,
    )


def near_kernel(count, own_ref, wqkv_ref, *refs):
    pieces, (stat_ref, mixed_ref, query_ref) = refs[:count], refs[count:]
    queries = split_heads(own_ref, wqkv_ref)
    query_ref[...] = queries
    top, total, mixed = fold_keys(pieces, queries, wqkv_ref, None)
    lane = lax.broadcasted_iota(jnp.int32, stat_ref.shape, 1)
    stat_ref[...] = jnp.where(lane == 0, top, total)
    mixed_ref[...] = mixed


def far_kernel(
    count, tokens_ref, query_ref, wqkv_ref, wout_ref, wclass_ref, labels_ref, stat_ref, mixed_ref,
    *refs,
):
    pieces, (state_ref, loss_ref) = refs[:count], refs[count:]
    chans = wqkv_ref.shape[0]
    here = tokens_ref.shape[0]
    state = (stat_ref[:, 0:1], stat_ref[:, 1:2], mixed_ref[...])
    _, total, mixed = fold_keys(pieces, query_ref[...], wqkv_ref, state)
    mixed = mixed / total
    lane = lax.broadcasted_iota(jnp.int32, (here, chans), 1)
    attended = jnp.zeros((here, chans), jnp.float32)
    for h in range(HEADS):
        attended = jnp.where(lane // HEAD_DIM == h, mixed[h * here : (h + 1) * here], attended)
    state = tokens_ref[...] + jnp.dot(
        attended.astype(jnp.bfloat16), wout_ref[...], preferred_element_type=jnp.float32
    )
    state_ref[...] = state.astype(jnp.bfloat16)
    class_in = layer_norm(state).astype(jnp.bfloat16)
    logits = lax.dot_general(
        class_in, wclass_ref[...], (((1,), (1,)), ((), ())), preferred_element_type=jnp.float32
    )
    top = jnp.max(logits, axis=1, keepdims=True)
    log_total = top + jnp.log(jnp.sum(jnp.exp(logits - top), axis=1, keepdims=True))
    number = lax.broadcasted_iota(jnp.int32, logits.shape, 1)
    label = to_column(labels_ref[...].reshape(1, here), here)
    picked = jnp.sum(jnp.where(number == label, logits, 0.0), axis=1, keepdims=True)
    loss = jnp.broadcast_to(log_total - picked, (here, here))
    same = lax.broadcasted_iota(jnp.int32, (here, here), 0) == lax.broadcasted_iota(
        jnp.int32, (here, here), 1
    )
    loss_ref[...] = jnp.sum(jnp.where(same, loss, 0.0), axis=0)


VM = pl.BlockSpec(memory_space=pltpu.VMEM)
HBM = pl.BlockSpec(memory_space=pltpu.HBM)


def params(mib=32):
    return pltpu.CompilerParams(vmem_limit_bytes=mib * 1024 * 1024)


def xor_permute(x, axis, mask, count):
    return lax.ppermute(x, axis, [(i, i ^ mask) for i in range(count)])


def exchange(groups, axis, bits, count):
    whole = groups[0] if len(groups) == 1 else jnp.concatenate(groups, axis=0)
    masks = [sum(1 << b for n, b in enumerate(bits) if m >> n & 1) for m in range(1, 1 << len(bits))]
    return [whole], [xor_permute(whole, axis, m, count) for m in masks]


def gather_stages():
    stages = []
    for axis in AXES:
        bits = list(range(lax.axis_size(axis).bit_length() - 1))[::-1]
        last = [bits.pop()] if axis == AXES[-1] else []
        stages += [(axis, bits[i : i + 2]) for i in range(0, len(bits), 2)]
        if last:
            stages.append((axis, last))
    return stages


def local(
    pixels, dw_kernel, dw_bias, norm_gain, w_expand, w_reduce, layer_scale, pixel_slot,
    intersection, parcel_pos, parcel_embed, attn_gain, w_qkv, w_out, w_class, labels,
):
    scenes, rows, width, chans = pixels.shape
    ksz = dw_kernel.shape[0]
    reach = ksz // 2
    slots = intersection.shape[1]
    owners = lax.axis_size("space") * lax.axis_size("scene")
    count = lax.axis_size("space")
    up = [(i, i + 1) for i in range(count - 1)]
    down = [(i + 1, i) for i in range(count - 1)]
    top = lax.ppermute(pixels[:, rows - reach :], "space", up)
    bottom = lax.ppermute(pixels[:, :reach], "space", down)

    part = rows // 2 * width

    def scratch(times):
        blocks = rows // 2 // BLOCK_ROWS
        return [
            pltpu.SemaphoreType.DMA((times, blocks)),
            pltpu.VMEM(
                (blocks, chans // LANES, BLOCK_ROWS + ksz - 1, width + 2 * MARGIN, LANES),
                jnp.float32,
            ),
            pltpu.VMEM((chans // LANES, part, LANES), jnp.float32),
            pltpu.VMEM((part, chans), jnp.float32),
            pltpu.VMEM(
                (blocks, part, w_expand.shape[1] // (blocks * (chans // LANES))), jnp.float32
            ),
            pltpu.VMEM((chans // LANES, ksz * ksz, TAP_ROWS, LANES), jnp.bfloat16),
            pltpu.VMEM((chans // LANES, 8, LANES), jnp.float32),
            pltpu.VMEM((times, rows // 2, width, chans), jnp.bfloat16),
        ]

    work = 2 * rows * width * chans * (ksz * ksz + 2 * w_expand.shape[1])
    zero_sums, zero_counts = pl.pallas_call(
        start_kernel,
        out_shape=(
            jax.ShapeDtypeStruct((slots, chans), jnp.float32),
            jax.ShapeDtypeStruct((slots, LANES), jnp.float32),
        ),
        out_specs=(VM, VM),
        compiler_params=params(8),
        cost_estimate=pl.CostEstimate(flops=START, bytes_accessed=1 << 20, transcendentals=0),
        name="start_sums",
    )()
    inputs = (
        pixels, pixel_slot, dw_kernel, dw_bias, norm_gain, w_expand, w_reduce, layer_scale,
        zero_sums, zero_counts, intersection, parcel_pos,
    )
    feats, sums, counts, normed, placer, local_rows = pl.pallas_call(
        functools.partial(inner_kernel, rows, slots, owners),
        out_shape=(
            jax.ShapeDtypeStruct(pixels.shape, jnp.bfloat16),
            jax.ShapeDtypeStruct((slots, chans), jnp.float32),
            jax.ShapeDtypeStruct((slots, LANES), jnp.float32),
            jax.ShapeDtypeStruct((part, chans), jnp.bfloat16),
            jax.ShapeDtypeStruct((CAP * owners, slots), jnp.float32),
            jax.ShapeDtypeStruct((slots, LANES), jnp.float32),
        ),
        in_specs=[VM] * len(inputs),
        out_specs=(HBM, VM, VM, VM, VM, VM),
        scratch_shapes=scratch(scenes),
        compiler_params=params(),
        cost_estimate=pl.CostEstimate(flops=work, bytes_accessed=6 << 20, transcendentals=0),
        name="inner_rows",
    )(*inputs)
    features, sent = pl.pallas_call(
        functools.partial(edge_kernel, rows, slots, owners),
        out_shape=(
            jax.ShapeDtypeStruct(pixels.shape, jnp.bfloat16),
            jax.ShapeDtypeStruct((owners, 1, CAP * chans + LANES), jnp.float32),
        ),
        in_specs=[VM] * 10 + [HBM] + [VM] * 5,
        out_specs=(HBM, VM),
        input_output_aliases={10: 0},
        scratch_shapes=scratch(scenes + 1)
        + [
            pltpu.VMEM((part, chans), jnp.bfloat16),
            pltpu.VMEM((slots, chans), jnp.float32),
            pltpu.VMEM((slots, LANES), jnp.float32),
        ],
        compiler_params=params(),
        cost_estimate=pl.CostEstimate(flops=work, bytes_accessed=6 << 20, transcendentals=0),
        name="edge_rows",
    )(
        pixels, top, bottom, pixel_slot, dw_kernel, dw_bias, norm_gain, w_expand, w_reduce,
        layer_scale, feats, sums, counts, normed, placer, local_rows,
    )
    arrived = lax.all_to_all(sent, AXES, split_axis=0, concat_axis=0, tiled=True)
    tokens, attn_in = pl.pallas_call(
        owner_kernel,
        out_shape=(
            jax.ShapeDtypeStruct((PAR_DEV, chans), jnp.float32),
            jax.ShapeDtypeStruct((PAR_DEV, chans), jnp.bfloat16),
        ),
        in_specs=[VM] * 3,
        out_specs=(VM, VM),
        compiler_params=params(),
        name="own_tokens",
    )(arrived, parcel_embed, attn_gain)
    held = [attn_in]
    stages = gather_stages()
    for axis, bits in stages[:-1]:
        kept, got = exchange(held, axis, bits, lax.axis_size(axis))
        held = kept + got
    axis, bits = stages[-1]
    far = [xor_permute(h, axis, 1 << bits[0], lax.axis_size(axis)) for h in held]
    heads = HEADS * PAR_DEV
    fold = 2 * owners * PAR_DEV * chans * (chans + heads)
    stat, mixed, queries = pl.pallas_call(
        functools.partial(near_kernel, len(held)),
        out_shape=(
            jax.ShapeDtypeStruct((heads, LANES), jnp.float32),
            jax.ShapeDtypeStruct((heads, chans), jnp.float32),
            jax.ShapeDtypeStruct((heads, chans), jnp.bfloat16),
        ),
        in_specs=[VM] * (2 + len(held)),
        out_specs=(VM,) * 3,
        compiler_params=params(),
        cost_estimate=pl.CostEstimate(flops=fold, bytes_accessed=2 << 20, transcendentals=0),
        name="near_keys",
    )(attn_in, w_qkv, *held)
    state, loss = pl.pallas_call(
        functools.partial(far_kernel, len(far)),
        out_shape=(
            jax.ShapeDtypeStruct((PAR_DEV, chans), jnp.bfloat16),
            jax.ShapeDtypeStruct((PAR_DEV,), jnp.float32),
        ),
        in_specs=[VM] * (8 + len(far)),
        out_specs=(VM, VM),
        compiler_params=params(),
        cost_estimate=pl.CostEstimate(flops=fold, bytes_accessed=2 << 20, transcendentals=0),
        name="far_keys",
    )(tokens, queries, w_qkv, w_out, w_class.T, labels, stat, mixed, *far)
    return features, state, loss


def solution(mesh):
    in_specs = (
        P("scene", "space", None, None),
        P(), P(), P(), P(), P(), P(),
        P("scene", "space", None),
        P(AXES, None),
        P(),
        P(AXES, None),
        P(), P(), P(), P(),
        P(AXES),
    )
    out_specs = (P("scene", "space", None, None), P(AXES, None), P(AXES))
    return jax.shard_map(local, mesh=mesh, in_specs=in_specs, out_specs=out_specs, check_vma=False)
```

```python
import functools

import jax
import jax.numpy as jnp
from jax import lax
from jax.experimental import pallas as pl
from jax.experimental.pallas import tpu as pltpu
from jax.sharding import PartitionSpec as P

CAP = 3
PAR_DEV = 64
HEADS = 6
HEAD_DIM = 64
BLOCK_ROWS = 4
MARGIN = 8
LANES = 128
EPS = 1e-06
TILE_COLS = 32
PIECE = 512
TAP_ROWS = 16
START = 1 << 34
AXES = ("space", "scene")
HIGHEST = lax.Precision.HIGHEST

def gelu(x):
    half = 0.5 * x
    return half + half * lax.erf(x * 0.5**0.5)


def layer_norm(values):
    average = jnp.mean(values, axis=-1, keepdims=True)
    centered = values - average
    return centered * lax.rsqrt(jnp.mean(centered * centered, axis=-1, keepdims=True) + EPS)


def to_column(row, rows):
    n = row.shape[1]
    same = lax.broadcasted_iota(jnp.int32, (n, n), 0) == lax.broadcasted_iota(jnp.int32, (n, n), 1)
    return jnp.sum(jnp.where(same, jnp.broadcast_to(row, (n, n)), 0), axis=1, keepdims=True)


def to_row(column):
    n = column.shape[0]
    same = lax.broadcasted_iota(jnp.int32, (n, n), 0) == lax.broadcasted_iota(jnp.int32, (n, n), 1)
    return jnp.sum(jnp.where(same, jnp.broadcast_to(column, (n, n)), 0), axis=0, keepdims=True)


def fill(windows, slab, width):
    for n, window in enumerate(windows):
        for i, row in enumerate(window):
            value = row().astype(jnp.float32)
            for cb in range(slab.shape[1]):
                slab[n, cb, i, MARGIN : MARGIN + width, :] = value[:, cb * LANES : (cb + 1) * LANES]


def conv_tile(n, cb, col, slab, spat, wb, bias_ref, width):
    ksz = dw_size(wb)
    start = MARGIN - ksz // 2 + col
    parts = range(0, TILE_COLS, TAP_ROWS)
    total = [[None for _ in parts] for _ in range(BLOCK_ROWS)]
    for i in range(slab.shape[2]):
        window = [
            [
                slab[n, cb, i, start + b + p : start + b + p + TAP_ROWS, :].astype(jnp.bfloat16)
                for b in range(ksz)
            ]
            for p in parts
        ]
        for a in range(ksz):
            r = i - a
            if not 0 <= r < BLOCK_ROWS:
                continue
            taps = [wb[cb, a * ksz + b] for b in range(ksz)]
            for k in range(len(window)):
                terms = [v * t for v, t in zip(window[k], taps)]
                while len(terms) > 1:
                    terms = [sum(terms[j + 1 : j + 2], terms[j]) for j in range(0, len(terms), 2)]
                term = terms[0].astype(jnp.float32)
                total[r][k] = term if total[r][k] is None else total[r][k] + term
    bias = bias_ref[cb, 0:1, :]
    for r in range(BLOCK_ROWS):
        for k, p in enumerate(parts):
            at = (n * BLOCK_ROWS + r) * width + col + p
            spat[cb, pl.ds(at, TAP_ROWS), :] = total[r][k] + bias


def dw_size(wb):
    return int(wb.shape[1] ** 0.5 + 0.5)


def norm_rows(spat, normed, gain_ref):
    values = jnp.concatenate([spat[cb] for cb in range(spat.shape[0])], axis=1)
    normed[...] = (layer_norm(values) * gain_ref[...].reshape(1, -1)).astype(jnp.bfloat16)


def rows_step(
    convolve, pointwise, slab, spat, normed, branch, ahead, wb, bias_ref, we_ref, wr_ref, width
):
    blocks, chan_blocks = slab.shape[:2]
    steps = blocks * chan_blocks
    chunk = we_ref.shape[1] // steps
    many = normed.shape[0]
    cols = list(range(0, width, TILE_COLS))

    def expand(part, slot, r):
        at = part * chunk
        ahead[slot, r : r + PIECE] = jnp.dot(
            normed[r : r + PIECE], we_ref[:, pl.ds(at, chunk)], preferred_element_type=jnp.float32
        )

    def reduce(part, slot, r):
        at = part * chunk
        branch[r : r + PIECE] += jnp.dot(
            gelu(ahead[slot, r : r + PIECE]).astype(jnp.bfloat16),
            wr_ref[pl.ds(at, chunk), :],
            preferred_element_type=jnp.float32,
        )

    def step(cb, carry):
        for n in range(blocks):
            part = cb * blocks + n
            todo = list(cols) if convolve else []
            for r in range(0, many, PIECE):
                if pointwise:
                    expand(min(part + 1, steps - 1), (n + 1) % blocks, r)
                    reduce(part, n, r)
                if todo:
                    conv_tile(n, cb, todo.pop(0), slab, spat, wb, bias_ref, width)
            for col in todo:
                conv_tile(n, cb, col, slab, spat, wb, bias_ref, width)
        return carry

    if pointwise:
        branch[...] = jnp.zeros_like(branch)
        for r in range(0, many, PIECE):
            expand(0, 0, r)
    for cb in range(chan_blocks):
        step(cb, 0)


def prepare(slab, wb, bias, dwk_ref, bias_ref, width):
    edge = jnp.zeros(slab.shape[:3] + (MARGIN, LANES), jnp.float32)
    slab[:, :, :, 0:MARGIN, :] = edge
    slab[:, :, :, MARGIN + width :, :] = edge
    values = bias_ref[...].reshape(1, -1)
    for cb in range(wb.shape[0]):
        bias[cb] = jnp.broadcast_to(values[:, cb * LANES : (cb + 1) * LANES], (8, LANES))
    ksz = dwk_ref.shape[0]
    for a in range(ksz):
        kernel = dwk_ref[a].astype(jnp.float32)
        for cb in range(wb.shape[0]):
            for b in range(ksz):
                wb[cb, a * ksz + b] = jnp.broadcast_to(
                    kernel[b : b + 1, cb * LANES : (cb + 1) * LANES], (TAP_ROWS, LANES)
                ).astype(jnp.bfloat16)


def pool(member, feats, sums_ref, counts_ref):
    sums_ref[...] += jnp.dot(member, feats, preferred_element_type=jnp.float32)
    ones = jnp.ones((member.shape[1], LANES), jnp.bfloat16)
    counts_ref[...] += jnp.dot(member, ones, preferred_element_type=jnp.float32)


def membership(slot_ref, scene, row0, many, width, slots):
    pieces = []
    for r in range(many):
        one = slot_ref[scene, row0 + r : row0 + r + 1, :]
        index = lax.broadcasted_iota(jnp.int32, (slots, width), 0)
        pieces.append((index == one).astype(jnp.float32).astype(jnp.bfloat16))
    return jnp.concatenate(pieces, axis=1)


def finish_rows(
    scene, starts, n, slots, width, x_ref, slot_ref, branch, scale_ref, feat_ref, sums_ref,
    counts_ref, feat_hbm, out_sems,
):
    size = BLOCK_ROWS * width
    center = jnp.concatenate(
        [x_ref[scene, r : r + BLOCK_ROWS].reshape(size, -1) for r in starts], axis=0
    )
    feats = (
        center.astype(jnp.float32) + scale_ref[...].reshape(1, -1) * branch[...]
    ).astype(jnp.bfloat16)
    feat_ref[n] = feats.reshape(len(starts) * BLOCK_ROWS, width, -1)
    writes = [
        pltpu.make_async_copy(
            feat_ref.at[n, pl.ds(k * BLOCK_ROWS, BLOCK_ROWS)],
            feat_hbm.at[scene, pl.ds(r, BLOCK_ROWS)],
            out_sems.at[n, k],
        )
        for k, r in enumerate(starts)
    ]
    for write in writes:
        write.start()
    member = jnp.concatenate(
        [membership(slot_ref, scene, r, BLOCK_ROWS, width, slots) for r in starts], axis=1
    )
    pool(member, feats, sums_ref, counts_ref)
    return writes


def window_rows(scene, row0, reach, rows, x_ref, top, bottom):
    source = []
    for r in range(row0 - reach, row0 + BLOCK_ROWS + reach):
        if r < 0:
            source.append(functools.partial(top, scene, r + reach))
        elif r >= rows:
            source.append(functools.partial(bottom, scene, r - rows))
        else:
            source.append(functools.partial(lambda r: x_ref[scene, r], r))
    return source


def start_kernel(sums_ref, counts_ref):
    sums_ref[...] = jnp.zeros_like(sums_ref)
    counts_ref[...] = jnp.zeros_like(counts_ref)


def route(owners, inter_ref, pos_ref, placer_ref, rows_ref):
    slots = inter_ref.shape[1]
    parcels = pos_ref.shape[0]
    listed = to_column(inter_ref[...], slots)
    number = lax.broadcasted_iota(jnp.int32, (slots, parcels), 1)
    position = jnp.sum(
        jnp.where(number == listed, jnp.broadcast_to(pos_ref[...].reshape(1, parcels), (slots, parcels)), 0),
        axis=1, keepdims=True,
    )
    owner = position // PAR_DEV
    owner_row = to_row(owner)
    this = lax.broadcasted_iota(jnp.int32, (slots, slots), 0)
    other = lax.broadcasted_iota(jnp.int32, (slots, slots), 1)
    rank = jnp.sum(
        jnp.where((owner == owner_row) & (other < this), 1, 0), axis=1, keepdims=True
    )
    place = to_row(rank * owners + owner)
    place_index = lax.broadcasted_iota(jnp.int32, (CAP * owners, slots), 0)
    placer_ref[...] = (place_index == place).astype(jnp.float32)
    local_row = (position - owner * PAR_DEV).astype(jnp.float32)
    rows_ref[...] = jnp.broadcast_to(local_row, rows_ref.shape)


def inner_kernel(
    rows, slots, owners, x_ref, slot_ref, dwk_ref, bias_ref, gain_ref, we_ref, wr_ref, scale_ref,
    sums_in, counts_in, inter_ref, pos_ref,
    feat_hbm, sums_ref, counts_ref, normed, placer_ref, rows_ref, out_sems, slab, spat, branch, ahead, wb, bias, feat_ref,
):
    scenes, _, width, _ = x_ref.shape
    reach = dw_size(wb) // 2
    sums_ref[...] = sums_in[...]
    counts_ref[...] = counts_in[...]
    route(owners, inter_ref, pos_ref, placer_ref, rows_ref)
    prepare(slab, wb, bias, dwk_ref, bias_ref, width)
    starts = range(BLOCK_ROWS, rows - BLOCK_ROWS, BLOCK_ROWS)
    writes = []
    for scene in range(scenes):
        fill(
            [window_rows(scene, r, reach, rows, x_ref, None, None) for r in starts], slab, width
        )
        rows_step(
            True, scene > 0, slab, spat, normed, branch, ahead, wb, bias, we_ref, wr_ref, width
        )
        if scene > 0:
            writes += finish_rows(
                scene - 1, starts, scene - 1, slots, width, x_ref, slot_ref, branch, scale_ref,
                feat_ref, sums_ref, counts_ref, feat_hbm, out_sems,
            )
        norm_rows(spat, normed, gain_ref)
    for write in writes:
        write.wait()


def edge_kernel(
    rows, slots, owners, x_ref, pair_ref, next_ref, slot_ref, dwk_ref, bias_ref, gain_ref, we_ref,
    wr_ref, scale_ref, feat_in, sums_in, counts_in, normed_in, placer_ref, rows_ref,
    feat_hbm, sent_ref, out_sems, slab, spat, branch, ahead, wb, bias, feat_ref, normed, sums_ref,
    counts_ref,
):
    scenes, _, width, _ = x_ref.shape
    reach = dw_size(wb) // 2
    sums_ref[...] = sums_in[...]
    counts_ref[...] = counts_in[...]
    normed[...] = normed_in[...]
    prepare(slab, wb, bias, dwk_ref, bias_ref, width)
    inside = range(BLOCK_ROWS, rows - BLOCK_ROWS, BLOCK_ROWS)
    outside = (0, rows - BLOCK_ROWS)
    even = lax.rem(lax.axis_index("space"), 2) == 0

    def halo(of_even, of_odd, scene, r):
        return jnp.where(
            even, of_even[scene, r].astype(jnp.float32), of_odd[scene, r].astype(jnp.float32)
        )

    top = functools.partial(halo, next_ref, pair_ref)
    bottom = functools.partial(halo, pair_ref, next_ref)
    writes = []
    for n in range(scenes + 1):
        if n < scenes:
            fill(
                [window_rows(n, r, reach, rows, x_ref, top, bottom) for r in outside],
                slab, width,
            )
        rows_step(
            n < scenes, True, slab, spat, normed, branch, ahead, wb, bias, we_ref, wr_ref, width
        )
        scene, starts = (scenes - 1, inside) if n == 0 else (n - 1, outside)
        writes += finish_rows(
            scene, starts, n, slots, width, x_ref, slot_ref, branch, scale_ref, feat_ref,
            sums_ref, counts_ref, feat_hbm, out_sems,
        )
        if n < scenes:
            norm_rows(spat, normed, gain_ref)
    placer = placer_ref[...]
    sent = jnp.dot(placer, sums_ref[...], precision=HIGHEST, preferred_element_type=jnp.float32)
    lane = lax.broadcasted_iota(jnp.int32, (slots, LANES), 1)
    counts_rows = jnp.where(lane < CAP, counts_ref[...], rows_ref[...])
    meta = jnp.dot(placer, counts_rows, precision=HIGHEST, preferred_element_type=jnp.float32)
    chans = sent.shape[1]
    lane = lax.broadcasted_iota(jnp.int32, (owners, LANES), 1)
    packed = jnp.zeros((owners, LANES), jnp.float32)
    for k in range(CAP):
        sent_ref[:, 0, k * chans : (k + 1) * chans] = sent[k * owners : (k + 1) * owners]
        packed = jnp.where(
            (lane == k) | (lane == CAP + k), meta[k * owners : (k + 1) * owners], packed
        )
    sent_ref[:, 0, CAP * chans :] = packed
    for write in writes:
        write.wait()


def owner_kernel(recv_ref, embed_ref, gain_ref, tokens_ref, attn_ref):
    chans = embed_ref.shape[1]
    meta = recv_ref[:, 0, CAP * chans :]
    tiles = recv_ref.shape[0]
    sums = jnp.zeros(tokens_ref.shape, jnp.float32)
    counts = jnp.zeros((PAR_DEV, LANES), jnp.float32)
    index = lax.broadcasted_iota(jnp.int32, (PAR_DEV, tiles), 0).astype(jnp.float32)
    for k in range(CAP):
        rows = jnp.broadcast_to(meta[:, CAP + k : CAP + k + 1], (tiles, LANES)).T[0:1, :]
        table = (index == rows).astype(jnp.float32)
        sums += jnp.dot(
            table, recv_ref[:, 0, k * chans : (k + 1) * chans],
            precision=HIGHEST, preferred_element_type=jnp.float32,
        )
        many = jnp.broadcast_to(meta[:, k : k + 1], (tiles, LANES))
        counts += jnp.dot(table, many, precision=HIGHEST, preferred_element_type=jnp.float32)
    tokens = sums / jnp.maximum(counts[:, :1], 1.0) + embed_ref[...].astype(jnp.float32)
    tokens_ref[...] = tokens
    attn_ref[...] = (layer_norm(tokens) * gain_ref[...].reshape(1, chans)).astype(jnp.bfloat16)


def fold_keys(pieces, queries, wqkv_ref, state):
    chans = wqkv_ref.shape[0]
    part = jnp.concatenate([p[...] for p in pieces], axis=0)
    keys = jnp.dot(
        part, wqkv_ref[:, chans : 2 * chans], preferred_element_type=jnp.float32
    ).astype(jnp.bfloat16)
    values = jnp.dot(
        part, wqkv_ref[:, 2 * chans :], preferred_element_type=jnp.float32
    ).astype(jnp.bfloat16)
    scores = lax.dot_general(
        queries, keys, (((1,), (1,)), ((), ())), preferred_element_type=jnp.float32
    )
    top = jnp.max(scores, axis=1, keepdims=True)
    if state is not None:
        top = jnp.maximum(state[0], top)
    weights = jnp.exp(scores - top)
    total = jnp.sum(weights, axis=1, keepdims=True)
    mixed = jnp.dot(weights.astype(jnp.bfloat16), values, preferred_element_type=jnp.float32)
    if state is not None:
        keep = jnp.exp(state[0] - top)
        total = total + keep * state[1]
        mixed = mixed + keep * state[2]
    return top, total, mixed


def split_heads(own_ref, wqkv_ref):
    chans = wqkv_ref.shape[0]
    queries = jnp.dot(
        own_ref[...], wqkv_ref[:, :chans], preferred_element_type=jnp.float32
    ) * HEAD_DIM ** (-0.5)
    lane = lax.broadcasted_iota(jnp.int32, queries.shape, 1)
    return jnp.concatenate(
        [jnp.where(lane // HEAD_DIM == h, queries, 0.0).astype(jnp.bfloat16) for h in range(HEADS)],
        axis=0,
    )


def near_kernel(count, own_ref, wqkv_ref, *refs):
    pieces, (stat_ref, mixed_ref, query_ref) = refs[:count], refs[count:]
    queries = split_heads(own_ref, wqkv_ref)
    query_ref[...] = queries
    top, total, mixed = fold_keys(pieces, queries, wqkv_ref, None)
    lane = lax.broadcasted_iota(jnp.int32, stat_ref.shape, 1)
    stat_ref[...] = jnp.where(lane == 0, top, total)
    mixed_ref[...] = mixed


def far_kernel(
    count, tokens_ref, query_ref, wqkv_ref, wout_ref, wclass_ref, labels_ref, stat_ref, mixed_ref,
    *refs,
):
    pieces, (state_ref, loss_ref) = refs[:count], refs[count:]
    chans = wqkv_ref.shape[0]
    here = tokens_ref.shape[0]
    state = (stat_ref[:, 0:1], stat_ref[:, 1:2], mixed_ref[...])
    _, total, mixed = fold_keys(pieces, query_ref[...], wqkv_ref, state)
    mixed = mixed / total
    lane = lax.broadcasted_iota(jnp.int32, (here, chans), 1)
    attended = jnp.zeros((here, chans), jnp.float32)
    for h in range(HEADS):
        attended = jnp.where(lane // HEAD_DIM == h, mixed[h * here : (h + 1) * here], attended)
    state = tokens_ref[...] + jnp.dot(
        attended.astype(jnp.bfloat16), wout_ref[...], preferred_element_type=jnp.float32
    )
    state_ref[...] = state.astype(jnp.bfloat16)
    class_in = layer_norm(state).astype(jnp.bfloat16)
    logits = lax.dot_general(
        class_in, wclass_ref[...], (((1,), (1,)), ((), ())), preferred_element_type=jnp.float32
    )
    top = jnp.max(logits, axis=1, keepdims=True)
    log_total = top + jnp.log(jnp.sum(jnp.exp(logits - top), axis=1, keepdims=True))
    number = lax.broadcasted_iota(jnp.int32, logits.shape, 1)
    label = to_column(labels_ref[...].reshape(1, here), here)
    picked = jnp.sum(jnp.where(number == label, logits, 0.0), axis=1, keepdims=True)
    loss = jnp.broadcast_to(log_total - picked, (here, here))
    same = lax.broadcasted_iota(jnp.int32, (here, here), 0) == lax.broadcasted_iota(
        jnp.int32, (here, here), 1
    )
    loss_ref[...] = jnp.sum(jnp.where(same, loss, 0.0), axis=0)


VM = pl.BlockSpec(memory_space=pltpu.VMEM)
HBM = pl.BlockSpec(memory_space=pltpu.HBM)


def params(mib=32):
    return pltpu.CompilerParams(vmem_limit_bytes=mib * 1024 * 1024)


def xor_permute(x, axis, mask, count):
    return lax.ppermute(x, axis, [(i, i ^ mask) for i in range(count)])


def exchange(groups, axis, bits, count):
    whole = groups[0] if len(groups) == 1 else jnp.concatenate(groups, axis=0)
    masks = [sum(1 << b for n, b in enumerate(bits) if m >> n & 1) for m in range(1, 1 << len(bits))]
    return [whole], [xor_permute(whole, axis, m, count) for m in masks]


def gather_stages():
    stages = []
    for axis in AXES:
        bits = list(range(lax.axis_size(axis).bit_length() - 1))[::-1]
        last = [bits.pop()] if axis == AXES[-1] else []
        stages += [(axis, bits[i : i + 2]) for i in range(0, len(bits), 2)]
        if last:
            stages.append((axis, last))
    return stages


def local(
    pixels, dw_kernel, dw_bias, norm_gain, w_expand, w_reduce, layer_scale, pixel_slot,
    intersection, parcel_pos, parcel_embed, attn_gain, w_qkv, w_out, w_class, labels,
):
    scenes, rows, width, chans = pixels.shape
    ksz = dw_kernel.shape[0]
    reach = ksz // 2
    slots = intersection.shape[1]
    owners = lax.axis_size("space") * lax.axis_size("scene")
    count = lax.axis_size("space")
    even = lax.rem(lax.axis_index("space"), 2) == 0
    head, tail = pixels[:, :reach], pixels[:, rows - reach :]
    pairs = [(i, i ^ 1) for i in range(count)]
    nexts = [(i, i + 1) for i in range(1, count - 1, 2)]
    nexts += [(j, i) for i, j in nexts]
    pair_halo = lax.ppermute(jnp.where(even, tail, head), "space", pairs)
    next_halo = lax.ppermute(jnp.where(even, head, tail), "space", nexts)

    part = rows // 2 * width

    def scratch(times):
        blocks = rows // 2 // BLOCK_ROWS
        return [
            pltpu.SemaphoreType.DMA((times, blocks)),
            pltpu.VMEM(
                (blocks, chans // LANES, BLOCK_ROWS + ksz - 1, width + 2 * MARGIN, LANES),
                jnp.float32,
            ),
            pltpu.VMEM((chans // LANES, part, LANES), jnp.float32),
            pltpu.VMEM((part, chans), jnp.float32),
            pltpu.VMEM(
                (blocks, part, w_expand.shape[1] // (blocks * (chans // LANES))), jnp.float32
            ),
            pltpu.VMEM((chans // LANES, ksz * ksz, TAP_ROWS, LANES), jnp.bfloat16),
            pltpu.VMEM((chans // LANES, 8, LANES), jnp.float32),
            pltpu.VMEM((times, rows // 2, width, chans), jnp.bfloat16),
        ]

    work = 2 * rows * width * chans * (ksz * ksz + 2 * w_expand.shape[1])
    zero_sums, zero_counts = pl.pallas_call(
        start_kernel,
        out_shape=(
            jax.ShapeDtypeStruct((slots, chans), jnp.float32),
            jax.ShapeDtypeStruct((slots, LANES), jnp.float32),
        ),
        out_specs=(VM, VM),
        compiler_params=params(8),
        cost_estimate=pl.CostEstimate(flops=START, bytes_accessed=1 << 20, transcendentals=0),
        name="start_sums",
    )()
    inputs = (
        pixels, pixel_slot, dw_kernel, dw_bias, norm_gain, w_expand, w_reduce, layer_scale,
        zero_sums, zero_counts, intersection, parcel_pos,
    )
    feats, sums, counts, normed, placer, local_rows = pl.pallas_call(
        functools.partial(inner_kernel, rows, slots, owners),
        out_shape=(
            jax.ShapeDtypeStruct(pixels.shape, jnp.bfloat16),
            jax.ShapeDtypeStruct((slots, chans), jnp.float32),
            jax.ShapeDtypeStruct((slots, LANES), jnp.float32),
            jax.ShapeDtypeStruct((part, chans), jnp.bfloat16),
            jax.ShapeDtypeStruct((CAP * owners, slots), jnp.float32),
            jax.ShapeDtypeStruct((slots, LANES), jnp.float32),
        ),
        in_specs=[VM] * len(inputs),
        out_specs=(HBM, VM, VM, VM, VM, VM),
        scratch_shapes=scratch(scenes),
        compiler_params=params(),
        cost_estimate=pl.CostEstimate(flops=work, bytes_accessed=6 << 20, transcendentals=0),
        name="inner_rows",
    )(*inputs)
    features, sent = pl.pallas_call(
        functools.partial(edge_kernel, rows, slots, owners),
        out_shape=(
            jax.ShapeDtypeStruct(pixels.shape, jnp.bfloat16),
            jax.ShapeDtypeStruct((owners, 1, CAP * chans + LANES), jnp.float32),
        ),
        in_specs=[VM] * 10 + [HBM] + [VM] * 5,
        out_specs=(HBM, VM),
        input_output_aliases={10: 0},
        scratch_shapes=scratch(scenes + 1)
        + [
            pltpu.VMEM((part, chans), jnp.bfloat16),
            pltpu.VMEM((slots, chans), jnp.float32),
            pltpu.VMEM((slots, LANES), jnp.float32),
        ],
        compiler_params=params(),
        cost_estimate=pl.CostEstimate(flops=work, bytes_accessed=6 << 20, transcendentals=0),
        name="edge_rows",
    )(
        pixels, pair_halo, next_halo, pixel_slot, dw_kernel, dw_bias, norm_gain, w_expand, w_reduce,
        layer_scale, feats, sums, counts, normed, placer, local_rows,
    )
    arrived = lax.all_to_all(sent, AXES, split_axis=0, concat_axis=0, tiled=True)
    tokens, attn_in = pl.pallas_call(
        owner_kernel,
        out_shape=(
            jax.ShapeDtypeStruct((PAR_DEV, chans), jnp.float32),
            jax.ShapeDtypeStruct((PAR_DEV, chans), jnp.bfloat16),
        ),
        in_specs=[VM] * 3,
        out_specs=(VM, VM),
        compiler_params=params(),
        name="own_tokens",
    )(arrived, parcel_embed, attn_gain)
    held = [attn_in]
    stages = gather_stages()
    for axis, bits in stages[:-1]:
        kept, got = exchange(held, axis, bits, lax.axis_size(axis))
        held = kept + got
    axis, bits = stages[-1]
    far = [xor_permute(h, axis, 1 << bits[0], lax.axis_size(axis)) for h in held]
    heads = HEADS * PAR_DEV
    fold = 2 * owners * PAR_DEV * chans * (chans + heads)
    stat, mixed, queries = pl.pallas_call(
        functools.partial(near_kernel, len(held)),
        out_shape=(
            jax.ShapeDtypeStruct((heads, LANES), jnp.float32),
            jax.ShapeDtypeStruct((heads, chans), jnp.float32),
            jax.ShapeDtypeStruct((heads, chans), jnp.bfloat16),
        ),
        in_specs=[VM] * (2 + len(held)),
        out_specs=(VM,) * 3,
        compiler_params=params(),
        cost_estimate=pl.CostEstimate(flops=fold, bytes_accessed=2 << 20, transcendentals=0),
        name="near_keys",
    )(attn_in, w_qkv, *held)
    state, loss = pl.pallas_call(
        functools.partial(far_kernel, len(far)),
        out_shape=(
            jax.ShapeDtypeStruct((PAR_DEV, chans), jnp.bfloat16),
            jax.ShapeDtypeStruct((PAR_DEV,), jnp.float32),
        ),
        in_specs=[VM] * (8 + len(far)),
        out_specs=(VM, VM),
        compiler_params=params(),
        cost_estimate=pl.CostEstimate(flops=fold, bytes_accessed=2 << 20, transcendentals=0),
        name="far_keys",
    )(tokens, queries, w_qkv, w_out, w_class.T, labels, stat, mixed, *far)
    return features, state, loss


def solution(mesh):
    in_specs = (
        P("scene", "space", None, None),
        P(), P(), P(), P(), P(), P(),
        P("scene", "space", None),
        P(AXES, None),
        P(),
        P(AXES, None),
        P(), P(), P(), P(),
        P(AXES),
    )
    out_specs = (P("scene", "space", None, None), P(AXES, None), P(AXES))
    return jax.shard_map(local, mesh=mesh, in_specs=in_specs, out_specs=out_specs, check_vma=False)
```

```python
import functools

import jax
import jax.numpy as jnp
from jax import lax
from jax.experimental import pallas as pl
from jax.experimental.pallas import tpu as pltpu
from jax.sharding import PartitionSpec as P

CAP = 3
PAR_DEV = 64
HEADS = 6
HEAD_DIM = 64
BLOCK_ROWS = 4
MARGIN = 8
LANES = 128
EPS = 1e-06
TILE_COLS = 32
PIECE = 512
TAP_ROWS = 16
START = 1 << 34
AXES = ("space", "scene")
HIGHEST = lax.Precision.HIGHEST

def gelu(x):
    half = 0.5 * x
    return half + half * lax.erf(x * 0.5**0.5)


def layer_norm(values):
    average = jnp.mean(values, axis=-1, keepdims=True)
    centered = values - average
    return centered * lax.rsqrt(jnp.mean(centered * centered, axis=-1, keepdims=True) + EPS)


def to_column(row, rows):
    n = row.shape[1]
    same = lax.broadcasted_iota(jnp.int32, (n, n), 0) == lax.broadcasted_iota(jnp.int32, (n, n), 1)
    return jnp.sum(jnp.where(same, jnp.broadcast_to(row, (n, n)), 0), axis=1, keepdims=True)


def to_row(column):
    n = column.shape[0]
    same = lax.broadcasted_iota(jnp.int32, (n, n), 0) == lax.broadcasted_iota(jnp.int32, (n, n), 1)
    return jnp.sum(jnp.where(same, jnp.broadcast_to(column, (n, n)), 0), axis=0, keepdims=True)


def fill(windows, slab, width):
    for n, window in enumerate(windows):
        for i, row in enumerate(window):
            value = row().astype(jnp.float32)
            for cb in range(slab.shape[1]):
                slab[n, cb, i, MARGIN : MARGIN + width, :] = value[:, cb * LANES : (cb + 1) * LANES]


def conv_tile(n, cb, col, slab, spat, wb, bias_ref, width):
    ksz = dw_size(wb)
    start = MARGIN - ksz // 2 + col
    parts = range(0, TILE_COLS, TAP_ROWS)
    total = [[None for _ in parts] for _ in range(BLOCK_ROWS)]
    for i in range(slab.shape[2]):
        window = [
            [
                slab[n, cb, i, start + b + p : start + b + p + TAP_ROWS, :].astype(jnp.bfloat16)
                for b in range(ksz)
            ]
            for p in parts
        ]
        for a in range(ksz):
            r = i - a
            if not 0 <= r < BLOCK_ROWS:
                continue
            taps = [wb[cb, a * ksz + b] for b in range(ksz)]
            for k in range(len(window)):
                terms = [v * t for v, t in zip(window[k], taps)]
                while len(terms) > 1:
                    terms = [sum(terms[j + 1 : j + 2], terms[j]) for j in range(0, len(terms), 2)]
                term = terms[0].astype(jnp.float32)
                total[r][k] = term if total[r][k] is None else total[r][k] + term
    bias = bias_ref[cb, 0:1, :]
    for r in range(BLOCK_ROWS):
        for k, p in enumerate(parts):
            at = (n * BLOCK_ROWS + r) * width + col + p
            spat[cb, pl.ds(at, TAP_ROWS), :] = total[r][k] + bias


def dw_size(wb):
    return int(wb.shape[1] ** 0.5 + 0.5)


def norm_rows(spat, normed, gain_ref):
    values = jnp.concatenate([spat[cb] for cb in range(spat.shape[0])], axis=1)
    normed[...] = (layer_norm(values) * gain_ref[...].reshape(1, -1)).astype(jnp.bfloat16)


def rows_step(
    convolve, pointwise, slab, spat, normed, branch, ahead, wb, bias_ref, we_ref, wr_ref, width
):
    blocks, chan_blocks = slab.shape[:2]
    steps = blocks * chan_blocks
    chunk = we_ref.shape[1] // steps
    many = normed.shape[0]
    cols = list(range(0, width, TILE_COLS))

    def expand(part, slot, r):
        at = part * chunk
        ahead[slot, r : r + PIECE] = jnp.dot(
            normed[r : r + PIECE], we_ref[:, pl.ds(at, chunk)], preferred_element_type=jnp.float32
        )

    def reduce(part, slot, r):
        at = part * chunk
        branch[r : r + PIECE] += jnp.dot(
            gelu(ahead[slot, r : r + PIECE]).astype(jnp.bfloat16),
            wr_ref[pl.ds(at, chunk), :],
            preferred_element_type=jnp.float32,
        )

    def step(cb, carry):
        for n in range(blocks):
            part = cb * blocks + n
            todo = list(cols) if convolve else []
            for r in range(0, many, PIECE):
                if todo:
                    conv_tile(n, cb, todo.pop(0), slab, spat, wb, bias_ref, width)
                if pointwise and part + 1 < steps:
                    expand(part + 1, (n + 1) % blocks, r)
                if pointwise:
                    reduce(part, n, r)
            for col in todo:
                conv_tile(n, cb, col, slab, spat, wb, bias_ref, width)
        return carry

    if pointwise:
        branch[...] = jnp.zeros_like(branch)
        for r in range(0, many, PIECE):
            expand(0, 0, r)
    for cb in range(chan_blocks):
        step(cb, 0)


def prepare(slab, wb, bias, dwk_ref, bias_ref, width):
    edge = jnp.zeros(slab.shape[:3] + (MARGIN, LANES), jnp.float32)
    slab[:, :, :, 0:MARGIN, :] = edge
    slab[:, :, :, MARGIN + width :, :] = edge
    values = bias_ref[...].reshape(1, -1)
    for cb in range(wb.shape[0]):
        bias[cb] = jnp.broadcast_to(values[:, cb * LANES : (cb + 1) * LANES], (8, LANES))
    ksz = dwk_ref.shape[0]
    for a in range(ksz):
        kernel = dwk_ref[a].astype(jnp.float32)
        for cb in range(wb.shape[0]):
            for b in range(ksz):
                wb[cb, a * ksz + b] = jnp.broadcast_to(
                    kernel[b : b + 1, cb * LANES : (cb + 1) * LANES], (TAP_ROWS, LANES)
                ).astype(jnp.bfloat16)


def pool(member, feats, sums_ref, counts_ref):
    sums_ref[...] += jnp.dot(member, feats, preferred_element_type=jnp.float32)
    ones = jnp.ones((member.shape[1], LANES), jnp.bfloat16)
    counts_ref[...] += jnp.dot(member, ones, preferred_element_type=jnp.float32)


def membership(slot_ref, scene, row0, many, width, slots):
    pieces = []
    for r in range(many):
        one = slot_ref[scene, row0 + r : row0 + r + 1, :]
        index = lax.broadcasted_iota(jnp.int32, (slots, width), 0)
        pieces.append((index == one).astype(jnp.float32).astype(jnp.bfloat16))
    return jnp.concatenate(pieces, axis=1)


def finish_rows(
    scene, starts, n, slots, width, x_ref, slot_ref, branch, scale_ref, feat_ref, sums_ref,
    counts_ref, feat_hbm, out_sems,
):
    size = BLOCK_ROWS * width
    center = jnp.concatenate(
        [x_ref[scene, r : r + BLOCK_ROWS].reshape(size, -1) for r in starts], axis=0
    )
    feats = (
        center.astype(jnp.float32) + scale_ref[...].reshape(1, -1) * branch[...]
    ).astype(jnp.bfloat16)
    feat_ref[n] = feats.reshape(len(starts) * BLOCK_ROWS, width, -1)
    writes = [
        pltpu.make_async_copy(
            feat_ref.at[n, pl.ds(k * BLOCK_ROWS, BLOCK_ROWS)],
            feat_hbm.at[scene, pl.ds(r, BLOCK_ROWS)],
            out_sems.at[n, k],
        )
        for k, r in enumerate(starts)
    ]
    for write in writes:
        write.start()
    member = jnp.concatenate(
        [membership(slot_ref, scene, r, BLOCK_ROWS, width, slots) for r in starts], axis=1
    )
    pool(member, feats, sums_ref, counts_ref)
    return writes


def window_rows(scene, row0, reach, rows, x_ref, top, bottom):
    source = []
    for r in range(row0 - reach, row0 + BLOCK_ROWS + reach):
        if r < 0:
            source.append(functools.partial(top, scene, r + reach))
        elif r >= rows:
            source.append(functools.partial(bottom, scene, r - rows))
        else:
            source.append(functools.partial(lambda r: x_ref[scene, r], r))
    return source


def start_kernel(sums_ref, counts_ref):
    sums_ref[...] = jnp.zeros_like(sums_ref)
    counts_ref[...] = jnp.zeros_like(counts_ref)


def route(owners, inter_ref, pos_ref, placer_ref, rows_ref):
    slots = inter_ref.shape[1]
    parcels = pos_ref.shape[0]
    listed = to_column(inter_ref[...], slots)
    number = lax.broadcasted_iota(jnp.int32, (slots, parcels), 1)
    position = jnp.sum(
        jnp.where(number == listed, jnp.broadcast_to(pos_ref[...].reshape(1, parcels), (slots, parcels)), 0),
        axis=1, keepdims=True,
    )
    owner = position // PAR_DEV
    owner_row = to_row(owner)
    this = lax.broadcasted_iota(jnp.int32, (slots, slots), 0)
    other = lax.broadcasted_iota(jnp.int32, (slots, slots), 1)
    rank = jnp.sum(
        jnp.where((owner == owner_row) & (other < this), 1, 0), axis=1, keepdims=True
    )
    place = to_row(rank * owners + owner)
    place_index = lax.broadcasted_iota(jnp.int32, (CAP * owners, slots), 0)
    placer_ref[...] = (place_index == place).astype(jnp.float32)
    local_row = (position - owner * PAR_DEV).astype(jnp.float32)
    rows_ref[...] = jnp.broadcast_to(local_row, rows_ref.shape)


def inner_kernel(
    rows, slots, owners, x_ref, slot_ref, dwk_ref, bias_ref, gain_ref, we_ref, wr_ref, scale_ref,
    sums_in, counts_in, inter_ref, pos_ref,
    feat_hbm, sums_ref, counts_ref, normed, placer_ref, rows_ref, out_sems, slab, spat, branch, ahead, wb, bias, feat_ref,
):
    scenes, _, width, _ = x_ref.shape
    reach = dw_size(wb) // 2
    sums_ref[...] = sums_in[...]
    counts_ref[...] = counts_in[...]
    route(owners, inter_ref, pos_ref, placer_ref, rows_ref)
    prepare(slab, wb, bias, dwk_ref, bias_ref, width)
    starts = range(BLOCK_ROWS, rows - BLOCK_ROWS, BLOCK_ROWS)
    writes = []
    for scene in range(scenes):
        fill(
            [window_rows(scene, r, reach, rows, x_ref, None, None) for r in starts], slab, width
        )
        rows_step(
            True, scene > 0, slab, spat, normed, branch, ahead, wb, bias, we_ref, wr_ref, width
        )
        if scene > 0:
            writes += finish_rows(
                scene - 1, starts, scene - 1, slots, width, x_ref, slot_ref, branch, scale_ref,
                feat_ref, sums_ref, counts_ref, feat_hbm, out_sems,
            )
        norm_rows(spat, normed, gain_ref)
    for write in writes:
        write.wait()


def edge_kernel(
    rows, slots, owners, x_ref, pair_ref, next_ref, slot_ref, dwk_ref, bias_ref, gain_ref, we_ref,
    wr_ref, scale_ref, feat_in, sums_in, counts_in, normed_in, placer_ref, rows_ref,
    feat_hbm, sent_ref, out_sems, slab, spat, branch, ahead, wb, bias, feat_ref, normed, sums_ref,
    counts_ref,
):
    scenes, _, width, _ = x_ref.shape
    reach = dw_size(wb) // 2
    sums_ref[...] = sums_in[...]
    counts_ref[...] = counts_in[...]
    normed[...] = normed_in[...]
    prepare(slab, wb, bias, dwk_ref, bias_ref, width)
    inside = range(BLOCK_ROWS, rows - BLOCK_ROWS, BLOCK_ROWS)
    outside = (0, rows - BLOCK_ROWS)
    even = lax.rem(lax.axis_index("space"), 2) == 0

    def halo(of_even, of_odd, scene, r):
        return jnp.where(
            even, of_even[scene, r].astype(jnp.float32), of_odd[scene, r].astype(jnp.float32)
        )

    top = functools.partial(halo, next_ref, pair_ref)
    bottom = functools.partial(halo, pair_ref, next_ref)
    writes = []
    for n in range(scenes + 1):
        if n < scenes:
            fill(
                [window_rows(n, r, reach, rows, x_ref, top, bottom) for r in outside],
                slab, width,
            )
        rows_step(
            n < scenes, True, slab, spat, normed, branch, ahead, wb, bias, we_ref, wr_ref, width
        )
        scene, starts = (scenes - 1, inside) if n == 0 else (n - 1, outside)
        writes += finish_rows(
            scene, starts, n, slots, width, x_ref, slot_ref, branch, scale_ref, feat_ref,
            sums_ref, counts_ref, feat_hbm, out_sems,
        )
        if n < scenes:
            norm_rows(spat, normed, gain_ref)
    placer = placer_ref[...]
    sent = jnp.dot(placer, sums_ref[...], precision=HIGHEST, preferred_element_type=jnp.float32)
    lane = lax.broadcasted_iota(jnp.int32, (slots, LANES), 1)
    counts_rows = jnp.where(lane < CAP, counts_ref[...], rows_ref[...])
    meta = jnp.dot(placer, counts_rows, precision=HIGHEST, preferred_element_type=jnp.float32)
    chans = sent.shape[1]
    lane = lax.broadcasted_iota(jnp.int32, (owners, LANES), 1)
    packed = jnp.zeros((owners, LANES), jnp.float32)
    for k in range(CAP):
        sent_ref[:, 0, k * chans : (k + 1) * chans] = sent[k * owners : (k + 1) * owners]
        packed = jnp.where(
            (lane == k) | (lane == CAP + k), meta[k * owners : (k + 1) * owners], packed
        )
    sent_ref[:, 0, CAP * chans :] = packed
    for write in writes:
        write.wait()


def owner_kernel(recv_ref, embed_ref, gain_ref, tokens_ref, attn_ref):
    chans = embed_ref.shape[1]
    meta = recv_ref[:, 0, CAP * chans :]
    tiles = recv_ref.shape[0]
    sums = jnp.zeros(tokens_ref.shape, jnp.float32)
    counts = jnp.zeros((PAR_DEV, LANES), jnp.float32)
    index = lax.broadcasted_iota(jnp.int32, (PAR_DEV, tiles), 0).astype(jnp.float32)
    for k in range(CAP):
        rows = jnp.broadcast_to(meta[:, CAP + k : CAP + k + 1], (tiles, LANES)).T[0:1, :]
        table = (index == rows).astype(jnp.float32)
        sums += jnp.dot(
            table, recv_ref[:, 0, k * chans : (k + 1) * chans],
            precision=HIGHEST, preferred_element_type=jnp.float32,
        )
        many = jnp.broadcast_to(meta[:, k : k + 1], (tiles, LANES))
        counts += jnp.dot(table, many, precision=HIGHEST, preferred_element_type=jnp.float32)
    tokens = sums / jnp.maximum(counts[:, :1], 1.0) + embed_ref[...].astype(jnp.float32)
    tokens_ref[...] = tokens
    attn_ref[...] = (layer_norm(tokens) * gain_ref[...].reshape(1, chans)).astype(jnp.bfloat16)


def fold_keys(pieces, queries, wqkv_ref, state):
    chans = wqkv_ref.shape[0]
    part = jnp.concatenate([p[...] for p in pieces], axis=0)
    keys = jnp.dot(
        part, wqkv_ref[:, chans : 2 * chans], preferred_element_type=jnp.float32
    ).astype(jnp.bfloat16)
    values = jnp.dot(
        part, wqkv_ref[:, 2 * chans :], preferred_element_type=jnp.float32
    ).astype(jnp.bfloat16)
    scores = lax.dot_general(
        queries, keys, (((1,), (1,)), ((), ())), preferred_element_type=jnp.float32
    )
    top = jnp.max(scores, axis=1, keepdims=True)
    if state is not None:
        top = jnp.maximum(state[0], top)
    weights = jnp.exp(scores - top)
    total = jnp.sum(weights, axis=1, keepdims=True)
    mixed = jnp.dot(weights.astype(jnp.bfloat16), values, preferred_element_type=jnp.float32)
    if state is not None:
        keep = jnp.exp(state[0] - top)
        total = total + keep * state[1]
        mixed = mixed + keep * state[2]
    return top, total, mixed


def split_heads(own_ref, wqkv_ref):
    chans = wqkv_ref.shape[0]
    queries = jnp.dot(
        own_ref[...], wqkv_ref[:, :chans], preferred_element_type=jnp.float32
    ) * HEAD_DIM ** (-0.5)
    lane = lax.broadcasted_iota(jnp.int32, queries.shape, 1)
    return jnp.concatenate(
        [jnp.where(lane // HEAD_DIM == h, queries, 0.0).astype(jnp.bfloat16) for h in range(HEADS)],
        axis=0,
    )


def near_kernel(count, own_ref, wqkv_ref, *refs):
    pieces, (stat_ref, mixed_ref, query_ref) = refs[:count], refs[count:]
    queries = split_heads(own_ref, wqkv_ref)
    query_ref[...] = queries
    top, total, mixed = fold_keys(pieces, queries, wqkv_ref, None)
    lane = lax.broadcasted_iota(jnp.int32, stat_ref.shape, 1)
    stat_ref[...] = jnp.where(lane == 0, top, total)
    mixed_ref[...] = mixed


def far_kernel(
    count, tokens_ref, query_ref, wqkv_ref, wout_ref, wclass_ref, labels_ref, stat_ref, mixed_ref,
    *refs,
):
    pieces, (state_ref, loss_ref) = refs[:count], refs[count:]
    chans = wqkv_ref.shape[0]
    here = tokens_ref.shape[0]
    state = (stat_ref[:, 0:1], stat_ref[:, 1:2], mixed_ref[...])
    _, total, mixed = fold_keys(pieces, query_ref[...], wqkv_ref, state)
    mixed = mixed / total
    lane = lax.broadcasted_iota(jnp.int32, (here, chans), 1)
    attended = jnp.zeros((here, chans), jnp.float32)
    for h in range(HEADS):
        attended = jnp.where(lane // HEAD_DIM == h, mixed[h * here : (h + 1) * here], attended)
    state = tokens_ref[...] + jnp.dot(
        attended.astype(jnp.bfloat16), wout_ref[...], preferred_element_type=jnp.float32
    )
    state_ref[...] = state.astype(jnp.bfloat16)
    class_in = layer_norm(state).astype(jnp.bfloat16)
    logits = lax.dot_general(
        class_in, wclass_ref[...], (((1,), (1,)), ((), ())), preferred_element_type=jnp.float32
    )
    top = jnp.max(logits, axis=1, keepdims=True)
    log_total = top + jnp.log(jnp.sum(jnp.exp(logits - top), axis=1, keepdims=True))
    number = lax.broadcasted_iota(jnp.int32, logits.shape, 1)
    label = to_column(labels_ref[...].reshape(1, here), here)
    picked = jnp.sum(jnp.where(number == label, logits, 0.0), axis=1, keepdims=True)
    loss = jnp.broadcast_to(log_total - picked, (here, here))
    same = lax.broadcasted_iota(jnp.int32, (here, here), 0) == lax.broadcasted_iota(
        jnp.int32, (here, here), 1
    )
    loss_ref[...] = jnp.sum(jnp.where(same, loss, 0.0), axis=0)


VM = pl.BlockSpec(memory_space=pltpu.VMEM)
HBM = pl.BlockSpec(memory_space=pltpu.HBM)


def params(mib=32):
    return pltpu.CompilerParams(vmem_limit_bytes=mib * 1024 * 1024)


def xor_permute(x, axis, mask, count):
    return lax.ppermute(x, axis, [(i, i ^ mask) for i in range(count)])


def exchange(groups, axis, bits, count):
    whole = groups[0] if len(groups) == 1 else jnp.concatenate(groups, axis=0)
    masks = [sum(1 << b for n, b in enumerate(bits) if m >> n & 1) for m in range(1, 1 << len(bits))]
    return [whole], [xor_permute(whole, axis, m, count) for m in masks]


def gather_stages():
    stages = []
    for axis in AXES:
        bits = list(range(lax.axis_size(axis).bit_length() - 1))[::-1]
        last = [bits.pop()] if axis == AXES[-1] else []
        stages += [(axis, bits[i : i + 2]) for i in range(0, len(bits), 2)]
        if last:
            stages.append((axis, last))
    return stages


def local(
    pixels, dw_kernel, dw_bias, norm_gain, w_expand, w_reduce, layer_scale, pixel_slot,
    intersection, parcel_pos, parcel_embed, attn_gain, w_qkv, w_out, w_class, labels,
):
    scenes, rows, width, chans = pixels.shape
    ksz = dw_kernel.shape[0]
    reach = ksz // 2
    slots = intersection.shape[1]
    owners = lax.axis_size("space") * lax.axis_size("scene")
    count = lax.axis_size("space")
    even = lax.rem(lax.axis_index("space"), 2) == 0
    head, tail = pixels[:, :reach], pixels[:, rows - reach :]
    pairs = [(i, i ^ 1) for i in range(count)]
    nexts = [(i, i + 1) for i in range(1, count - 1, 2)]
    nexts += [(j, i) for i, j in nexts]
    pair_halo = lax.ppermute(jnp.where(even, tail, head), "space", pairs)
    next_halo = lax.ppermute(jnp.where(even, head, tail), "space", nexts)

    part = rows // 2 * width

    def scratch(times):
        blocks = rows // 2 // BLOCK_ROWS
        return [
            pltpu.SemaphoreType.DMA((times, blocks)),
            pltpu.VMEM(
                (blocks, chans // LANES, BLOCK_ROWS + ksz - 1, width + 2 * MARGIN, LANES),
                jnp.float32,
            ),
            pltpu.VMEM((chans // LANES, part, LANES), jnp.float32),
            pltpu.VMEM((part, chans), jnp.float32),
            pltpu.VMEM(
                (blocks, part, w_expand.shape[1] // (blocks * (chans // LANES))), jnp.float32
            ),
            pltpu.VMEM((chans // LANES, ksz * ksz, TAP_ROWS, LANES), jnp.bfloat16),
            pltpu.VMEM((chans // LANES, 8, LANES), jnp.float32),
            pltpu.VMEM((times, rows // 2, width, chans), jnp.bfloat16),
        ]

    work = 2 * rows * width * chans * (ksz * ksz + 2 * w_expand.shape[1])
    zero_sums, zero_counts = pl.pallas_call(
        start_kernel,
        out_shape=(
            jax.ShapeDtypeStruct((slots, chans), jnp.float32),
            jax.ShapeDtypeStruct((slots, LANES), jnp.float32),
        ),
        out_specs=(VM, VM),
        compiler_params=params(8),
        cost_estimate=pl.CostEstimate(flops=START, bytes_accessed=1 << 20, transcendentals=0),
        name="start_sums",
    )()
    inputs = (
        pixels, pixel_slot, dw_kernel, dw_bias, norm_gain, w_expand, w_reduce, layer_scale,
        zero_sums, zero_counts, intersection, parcel_pos,
    )
    feats, sums, counts, normed, placer, local_rows = pl.pallas_call(
        functools.partial(inner_kernel, rows, slots, owners),
        out_shape=(
            jax.ShapeDtypeStruct(pixels.shape, jnp.bfloat16),
            jax.ShapeDtypeStruct((slots, chans), jnp.float32),
            jax.ShapeDtypeStruct((slots, LANES), jnp.float32),
            jax.ShapeDtypeStruct((part, chans), jnp.bfloat16),
            jax.ShapeDtypeStruct((CAP * owners, slots), jnp.float32),
            jax.ShapeDtypeStruct((slots, LANES), jnp.float32),
        ),
        in_specs=[VM] * len(inputs),
        out_specs=(HBM, VM, VM, VM, VM, VM),
        scratch_shapes=scratch(scenes),
        compiler_params=params(),
        cost_estimate=pl.CostEstimate(flops=work, bytes_accessed=6 << 20, transcendentals=0),
        name="inner_rows",
    )(*inputs)
    features, sent = pl.pallas_call(
        functools.partial(edge_kernel, rows, slots, owners),
        out_shape=(
            jax.ShapeDtypeStruct(pixels.shape, jnp.bfloat16),
            jax.ShapeDtypeStruct((owners, 1, CAP * chans + LANES), jnp.float32),
        ),
        in_specs=[VM] * 10 + [HBM] + [VM] * 5,
        out_specs=(HBM, VM),
        input_output_aliases={10: 0},
        scratch_shapes=scratch(scenes + 1)
        + [
            pltpu.VMEM((part, chans), jnp.bfloat16),
            pltpu.VMEM((slots, chans), jnp.float32),
            pltpu.VMEM((slots, LANES), jnp.float32),
        ],
        compiler_params=params(),
        cost_estimate=pl.CostEstimate(flops=work, bytes_accessed=6 << 20, transcendentals=0),
        name="edge_rows",
    )(
        pixels, pair_halo, next_halo, pixel_slot, dw_kernel, dw_bias, norm_gain, w_expand, w_reduce,
        layer_scale, feats, sums, counts, normed, placer, local_rows,
    )
    arrived = lax.all_to_all(sent, AXES, split_axis=0, concat_axis=0, tiled=True)
    tokens, attn_in = pl.pallas_call(
        owner_kernel,
        out_shape=(
            jax.ShapeDtypeStruct((PAR_DEV, chans), jnp.float32),
            jax.ShapeDtypeStruct((PAR_DEV, chans), jnp.bfloat16),
        ),
        in_specs=[VM] * 3,
        out_specs=(VM, VM),
        compiler_params=params(),
        name="own_tokens",
    )(arrived, parcel_embed, attn_gain)
    held = [attn_in]
    stages = gather_stages()
    for axis, bits in stages[:-1]:
        kept, got = exchange(held, axis, bits, lax.axis_size(axis))
        held = kept + got
    axis, bits = stages[-1]
    far = [xor_permute(h, axis, 1 << bits[0], lax.axis_size(axis)) for h in held]
    heads = HEADS * PAR_DEV
    fold = 2 * owners * PAR_DEV * chans * (chans + heads)
    stat, mixed, queries = pl.pallas_call(
        functools.partial(near_kernel, len(held)),
        out_shape=(
            jax.ShapeDtypeStruct((heads, LANES), jnp.float32),
            jax.ShapeDtypeStruct((heads, chans), jnp.float32),
            jax.ShapeDtypeStruct((heads, chans), jnp.bfloat16),
        ),
        in_specs=[VM] * (2 + len(held)),
        out_specs=(VM,) * 3,
        compiler_params=params(),
        cost_estimate=pl.CostEstimate(flops=fold, bytes_accessed=2 << 20, transcendentals=0),
        name="near_keys",
    )(attn_in, w_qkv, *held)
    state, loss = pl.pallas_call(
        functools.partial(far_kernel, len(far)),
        out_shape=(
            jax.ShapeDtypeStruct((PAR_DEV, chans), jnp.bfloat16),
            jax.ShapeDtypeStruct((PAR_DEV,), jnp.float32),
        ),
        in_specs=[VM] * (8 + len(far)),
        out_specs=(VM, VM),
        compiler_params=params(),
        cost_estimate=pl.CostEstimate(flops=fold, bytes_accessed=2 << 20, transcendentals=0),
        name="far_keys",
    )(tokens, queries, w_qkv, w_out, w_class.T, labels, stat, mixed, *far)
    return features, state, loss


def solution(mesh):
    in_specs = (
        P("scene", "space", None, None),
        P(), P(), P(), P(), P(), P(),
        P("scene", "space", None),
        P(AXES, None),
        P(),
        P(AXES, None),
        P(), P(), P(), P(),
        P(AXES),
    )
    out_specs = (P("scene", "space", None, None), P(AXES, None), P(AXES))
    return jax.shard_map(local, mesh=mesh, in_specs=in_specs, out_specs=out_specs, check_vma=False)
```
